128 devices in a mesh: dp: 32 (over y, z, core), tensor: 4 (over x).
Axes of the slice: x: 4, y: 4, z: 4, core: 2. Of those that a mesh axis runs over, the one named last changes fastest.
Arguments:
- history: bfloat16 [9, 8192, 2048], P(None, 'dp'), may hold values from -6 to 6
- lengths: int32 [32], P('dp'), may hold values from 1 to 256, 4915 in all
- cotangent: bfloat16 [8192, 2048], P('dp'), may hold values from -6 to 6
- w_qkv: bfloat16 [2048, 3, 2048], P(None, None, 'tensor'), may hold values from -0.125 to 0.125
- b_qkv: float32 [3, 2048], P(None, 'tensor'), may hold values from -4 to 4
- w_out: bfloat16 [2048, 2048], P('tensor'), may hold values from -0.75 to 0.75
- w_fc1: bfloat16 [2048, 8192], P(None, 'tensor'), may hold values from -0.125 to 0.125
- b_fc1: float32 [8192], P('tensor'), may hold values from -6 to 6
- w_fc2: bfloat16 [8192, 2048], P('tensor'), may hold values from -0.0625 to 0.0625
- out_bias: float32 [2048], replicated, may hold values from -4 to 4
- norm_gain: float32 [4, 2048], replicated, may hold values from 0.25 to 1.75
- norm_bias: float32 [4, 2048], replicated, may hold values from -4 to 4
- mix_gain: float32 [2048], replicated, may hold values from 0.25 to 1.75
- mix_in: float32 [2048, 36], replicated, may hold values from -0.125 to 0.125
- mix_out: float32 [36, 36], replicated, may hold values from -1 to 1
- mix_bias: float32 [36], replicated, may hold values from -0.5 to 1
Outputs:
- block_out: bfloat16 [8192, 2048], P('dp')
- grad_history: bfloat16 [9, 8192, 2048], P(None, ('dp', 'tensor'))
- grad_w_qkv: float32 [2048, 3, 2048], P('dp', None, 'tensor')
- grad_b_qkv: float32 [3, 2048], replicated
- grad_w_out: float32 [2048, 2048], P('tensor', 'dp')
- grad_w_fc1: float32 [2048, 8192], P('dp', 'tensor')
- grad_b_fc1: float32 [8192], replicated
- grad_w_fc2: float32 [8192, 2048], P('tensor', 'dp')
- grad_out_bias: float32 [2048], replicated
- grad_norm_gain: float32 [4, 2048], replicated
- grad_norm_bias: float32 [4, 2048], replicated
- grad_mix_gain: float32 [2048], replicated
- grad_mix_in: float32 [2048, 36], replicated
- grad_mix_out: float32 [36, 36], replicated
- grad_mix_bias: float32 [36], replicated
The draws below stay inside these ranges and needn't reach their ends.
Inputs may be any that keep to these rules, and one draw needn't show every extreme that they name: `lengths`: valid tokens of each sequence; the other slots of its 256 are padding.
All inputs are finite; a program needn't handle non-finite values. No bound on the sum of `lengths` on one device may be relied on, other than what follows from the above.
Results may differ from the reference program's by a relative error of at most 0.012.
The reference program's roundings to bfloat16 on the way count: a program that leaves them out, or rounds other values in their place, can miss the bound.
Values sent between devices are 32-bit elements; how exact they have to be, the bound alone decides.
No kernel may reach another device: no remote copies, remote signals or barrier semaphores. Data moves between devices by JAX's collectives and lax.ppermute only.
A program may use at most 320 MiB of HBM per device.

```python
import math
import jax
import jax.numpy as jnp
import numpy as np
from jax import lax

D = 2048
HEADS = 16
HD = 128
FF = 8192
ROT = 32
HIST = 9
STREAMS = 4
MIXH = 36
SEQ_LEN = 256
NSEQ = 32
TOKENS = 8192
N_DP = 32


def level_of(stream_key, shape, split, smallest, high):
    def one(axis_at, parts):
        draws = jax.random.uniform(jax.random.fold_in(jax.random.fold_in(stream_key, 6), axis_at), (parts,), jnp.float32, smallest / len(split), high / len(split))
        return jnp.repeat(jnp.exp(draws), shape[axis_at] // parts).reshape((-1,) + (1,) * (len(shape) - axis_at - 1))

    loudness = one(*split[0])
    for cut in split[1:]:
        loudness = loudness * one(*cut)
    return loudness


def split_up(count, total, most, lean):
    portions = [(1 << 20) // math.isqrt(grade ** lean) + 1 for grade in range(2, count + 1)]
    surplus, given = total - most - (count - 1), [1] * (count - 1)
    while surplus > 0:
        candidates = [i for i in range(count - 1) if given[i] < most]
        whole, budget = sum([portions[i] for i in candidates]), surplus
        for i in candidates:
            addition = min(most - given[i], max(1, budget * portions[i] // whole), surplus)
            given[i] = given[i] + addition
            surplus = surplus - addition
    return np.array([most] + given)


def uneven(key, amount, total, limit, lean):
    if amount == 2:
        one = jax.random.randint(key, (), max(1, total - limit), min(limit, total - 1) + 1)
        return jnp.stack([one, total - one])
    tallies = jnp.asarray(split_up(amount, total, limit, lean), jnp.int32)
    couples = (amount - 1) // 2
    giver, sink = tallies[1:1 + 2 * couples:2], tallies[2:2 + 2 * couples:2]
    room = jnp.minimum(giver - 1, limit - sink)
    passed = jax.random.randint(jax.random.fold_in(key, 1), (couples,), 0, 1 << 20) % (room + 1)
    tallies = tallies.at[1:1 + 2 * couples:2].set(giver - passed).at[2:2 + 2 * couples:2].set(sink + passed)
    return tallies[jax.random.permutation(jax.random.fold_in(key, 2), amount)]


def scatter_about(own_key, dims, scale, bound, pieces=(), held_as=jnp.bfloat16):
    loudness = level_of(own_key, dims, pieces, -0.22, 0.18) if pieces else 1.0
    drawn = jax.random.normal(own_key, dims, jnp.float32) * scale * loudness
    return jnp.minimum(jnp.maximum(drawn, -bound), bound).astype(held_as)


def setup_inputs(seed: int = 0) -> dict:
    streams_of = jax.random.split(jax.random.key(seed), 17)
    history = scatter_about(streams_of[0], (HIST, TOKENS, D), 1.0, 6.0, ((1, 32),))
    lengths = uneven(streams_of[1], NSEQ, N_DP * SEQ_LEN * 3 // 5, SEQ_LEN, 2).astype(jnp.int32)
    cotangent = scatter_about(streams_of[2], (TOKENS, D), 1.0, 6.0, ((0, 32),))
    w_qkv = scatter_about(streams_of[3], (D, 3, D), D ** -0.5, 0.125, ((2, 4),))
    b_qkv = scatter_about(streams_of[4], (3, D), 0.3, 4.0, ((1, 4),), jnp.float32)
    w_out = scatter_about(streams_of[5], (D, D), (D // 32) ** -0.5, 0.75, ((0, 4),))
    w_fc1 = scatter_about(streams_of[6], (D, FF), D ** -0.5, 0.125, ((1, 4),))
    b_fc1 = scatter_about(streams_of[7], (FF,), 0.5, 6.0, ((0, 4),), jnp.float32)
    w_fc2 = scatter_about(streams_of[8], (FF, D), FF ** -0.5, 0.0625, ((0, 4),))
    out_bias = scatter_about(streams_of[9], (D,), 0.3, 4.0, (), jnp.float32)
    norm_gain = jnp.clip(1.0 + 0.15 * jax.random.normal(streams_of[10], (STREAMS, D), jnp.float32), 0.25, 1.75)
    norm_bias = scatter_about(streams_of[11], (STREAMS, D), 0.3, 4.0, (), jnp.float32)
    mix_gain = jnp.clip(1.0 + 0.15 * jax.random.normal(streams_of[12], (D,), jnp.float32), 0.25, 1.75)
    mix_in = scatter_about(streams_of[13], (D, MIXH), D ** -0.5, 0.125, (), jnp.float32)
    mix_out = scatter_about(streams_of[14], (MIXH, MIXH), MIXH ** -0.5, 1.0, (), jnp.float32)
    mix_bias = jnp.clip(jax.random.uniform(streams_of[15], (MIXH,), jnp.float32, -0.5, 1.0), -0.5, 1.0)
    return {"history": history, "lengths": lengths, "cotangent": cotangent, "w_qkv": w_qkv, "b_qkv": b_qkv, "w_out": w_out, "w_fc1": w_fc1, "b_fc1": b_fc1, "w_fc2": w_fc2, "out_bias": out_bias, "norm_gain": norm_gain, "norm_bias": norm_bias, "mix_gain": mix_gain, "mix_in": mix_in, "mix_out": mix_out, "mix_bias": mix_bias}


HIGH = lax.Precision.HIGHEST

@jax.custom_vjp
def low(v):
    return lax.optimization_barrier(v.astype(jnp.bfloat16)).astype(jnp.float32)

@jax.custom_vjp
def low_back(v):
    return v

def low_keep(v):
    return (low(v), None)

def low_pass(kept, grad):
    return (grad,)

def back_keep(v):
    return (v, None)

def back_low(kept, grad):
    return (low(grad),)
low.defvjp(low_keep, low_pass)
low_back.defvjp(back_keep, back_low)

def rotary_tables(length):
    position = jnp.arange(length, dtype=jnp.float32)
    freq_steps = jnp.arange(0, ROT, 2, dtype=jnp.float32) / ROT
    inverse = jnp.exp(freq_steps * -math.log(10000.0))
    angles = position[:, None] * inverse[None, :]
    cosine = jnp.concatenate([jnp.cos(angles), jnp.cos(angles)], -1)[:, None, :]
    sine_table = jnp.concatenate([jnp.sin(angles), jnp.sin(angles)], -1)[:, None, :]
    return (cosine, sine_table)

def rotate(heads_in, cosine, sine_table):
    turning = heads_in[..., :ROT]
    lead_half = turning[..., :ROT // 2]
    tail_half = turning[..., ROT // 2:]
    swapped = jnp.concatenate([-tail_half, lead_half], -1)
    return jnp.concatenate([turning * cosine + swapped * sine_table, heads_in[..., ROT:]], -1)

def attend(block):
    queries, key_heads, value_heads, length = block
    position = jnp.arange(SEQ_LEN, dtype=jnp.int32)
    scores = jnp.einsum('qhe,khe->hqk', queries, key_heads, precision=HIGH) * (1.0 / math.sqrt(HD))
    scores = low_back(scores)
    allowed = (position[None, :] <= position[:, None]) & (position[None, :] < length)
    scores = jnp.where(allowed[None], scores, -1e+30)
    row_top = lax.optimization_barrier(jnp.max(scores, -1, keepdims=True))
    weights = jnp.exp(scores - row_top)
    attn_probs = weights / lax.optimization_barrier(jnp.sum(weights, -1, keepdims=True))
    probs_low = low(attn_probs)
    return jnp.einsum('hqk,khe->qhe', probs_low, value_heads, precision=HIGH)

def forward(history, w_qkv, b_qkv, w_out, w_fc1, b_fc1, w_fc2, out_bias, norm_gain, norm_bias, mix_gain, mix_in, mix_out, mix_bias, valid_rows, lengths):
    current = history[HIST - 1]
    mix_norm = current * lax.rsqrt(lax.optimization_barrier(jnp.mean(current * current, -1, keepdims=True)) + 1e-06) * mix_gain
    mix_hidden = jax.nn.gelu(jnp.dot(mix_norm, mix_in, precision=HIGH), approximate=False)
    mix_weight = (jnp.dot(mix_hidden, mix_out, precision=HIGH) + mix_bias).reshape(TOKENS, STREAMS, HIST)
    streams = jnp.einsum('tcj,jtd->ctd', mix_weight, history, precision=HIGH)
    row_mean = lax.optimization_barrier(jnp.mean(streams, -1, keepdims=True))
    centered = streams - row_mean
    row_var = lax.optimization_barrier(jnp.mean(centered * centered, -1, keepdims=True))
    normed = low(centered * lax.rsqrt(row_var + 1e-05) * norm_gain[:, None, :] + norm_bias[:, None, :])
    projected = jnp.einsum('ctd,dce->cte', normed[:3], w_qkv, precision=HIGH) + b_qkv[:, None, :]
    projected = low_back(projected).reshape(3, NSEQ, SEQ_LEN, HEADS, HD)
    cosine, sine_table = rotary_tables(SEQ_LEN)
    queries = low(rotate(projected[0], cosine, sine_table))
    key_heads = low(rotate(projected[1], cosine, sine_table))
    value_heads = low(projected[2])
    context = lax.map(jax.checkpoint(attend), (queries, key_heads, value_heads, lengths))
    context = low(low_back(context)).reshape(TOKENS, D)
    attn_branch = jnp.dot(context, w_out, precision=HIGH)
    hidden_pre = low_back(jnp.dot(normed[3], w_fc1, precision=HIGH) + b_fc1)
    activation = low(jax.nn.gelu(hidden_pre, approximate=False))
    ffn_branch = jnp.dot(activation, w_fc2, precision=HIGH)
    return streams[3] + valid_rows * (attn_branch + ffn_branch + out_bias)

def reference(history, lengths, cotangent, w_qkv, b_qkv, w_out, w_fc1, b_fc1, w_fc2, out_bias, norm_gain, norm_bias, mix_gain, mix_in, mix_out, mix_bias):
    position = jnp.arange(SEQ_LEN, dtype=jnp.int32)
    valid_rows = (position[None, :] < lengths[:, None]).astype(jnp.float32).reshape(TOKENS, 1)
    params = tuple((item.astype(jnp.float32) for item in (history, w_qkv, b_qkv, w_out, w_fc1, b_fc1, w_fc2, out_bias, norm_gain, norm_bias, mix_gain, mix_in, mix_out, mix_bias)))

    def wrapped(*primal):
        return forward(*primal, valid_rows, lengths)
    output, pullback = jax.vjp(wrapped, *params)
    gradients = pullback(cotangent.astype(jnp.float32))
    return (output.astype(jnp.bfloat16), gradients[0].astype(jnp.bfloat16), gradients[1], gradients[2], gradients[3], gradients[4], gradients[5], gradients[6], gradients[7], gradients[8], gradients[9], gradients[10], gradients[11], gradients[12], gradients[13])
```

```python
import functools
import math

import jax
import jax.numpy as jnp
import numpy as np
from jax import lax
from jax.experimental import pallas as pl
from jax.experimental.pallas import tpu as pltpu
from jax.sharding import PartitionSpec as P

D = 2048
HD = 128
ROT = 32
HIST = 9
STREAMS = 4
MIXH = 36
SEQ = 256
QUARTER = 64
F32 = jnp.float32
BF16 = jnp.bfloat16
HIGH = lax.Precision.HIGHEST
ROWS_COLS = (((1,), (1,)), ((), ()))
ROWS_ROWS = (((0,), (0,)), ((), ()))
ALL = ("dp", "tensor")


def place():
    dp = lax.axis_index("dp")
    return dp // 8, (dp // 2) % 4, dp % 2, lax.axis_index("tensor")


def dp_of(y, z, c):
    return ((y % 4) * 4 + z % 4) * 2 + c


def yz_pairs(step, phase):
    out = []
    for y in range(4):
        for z in range(4):
            for c in range(2):
                along_y = c == phase
                to = dp_of(y + step, z, c) if along_y else dp_of(y, z + step, c)
                out.append((dp_of(y, z, c), to))
    return out


def x_pairs():
    out = []
    for d in range(32):
        for x in range(4):
            out.append((d * 4 + x, d * 4 + (x + (1 if d % 2 == 0 else 3)) % 4))
    return out


def to_yz(a, step, phase):
    return lax.ppermute(a, "dp", yz_pairs(step, phase))


def to_x(a):
    return lax.ppermute(a, ALL, x_pairs())


def to_mate(a):
    return lax.ppermute(a, "dp", [(d, d ^ 1) for d in range(32)])


def x_chunk(c, x, r):
    return jnp.where(c == 0, x - r + 4, x + r) % 4


def gelu_parts(v):
    cdf = 0.5 * (1.0 + lax.erf(v * math.sqrt(0.5)))
    pdf = jnp.exp(-0.5 * v * v) * (1.0 / math.sqrt(2.0 * math.pi))
    return v * cdf, cdf + v * pdf


def rounded(v):
    return v.astype(BF16).astype(F32)


VMEM = pl.BlockSpec(memory_space=pltpu.VMEM)
SMEM = pl.BlockSpec(memory_space=pltpu.SMEM)
ANY = pl.BlockSpec(memory_space=pl.ANY)
HBM = pl.BlockSpec(memory_space=pltpu.HBM)


COST = {}


def call(name, kernel, in_specs, out_shape, args, after=(), scratch=(), grid=(), out_specs=None, mib=16, aliases=None):
    n_in, n_after = len(in_specs), len(after)

    def body(*refs):
        kernel(*refs[:n_in], *refs[n_in + n_after :])

    if out_specs is None:
        out_specs = jax.tree.map(lambda _: VMEM, out_shape)
    return pl.pallas_call(
        body,
        name=name,
        grid=grid,
        in_specs=list(in_specs) + [ANY] * n_after,
        out_specs=out_specs,
        scratch_shapes=list(scratch),
        out_shape=out_shape,
        input_output_aliases=aliases or {},
        compiler_params=pltpu.CompilerParams(vmem_limit_bytes=mib * 1024 * 1024),
        cost_estimate=pl.CostEstimate(
            flops=int(COST.get(name, 1.0) * 1e9), bytes_accessed=1, transcendentals=0
        ),
    )(*args, *after)


def held(a):
    return pltpu.with_memory_space_constraint(a, pltpu.HBM)


def whole(shape):
    return pl.BlockSpec(shape, lambda *_: (0,) * len(shape))


def shaped(shape, dtype=F32):
    return jax.ShapeDtypeStruct(shape, dtype)


def split_in_three(w):
    pad = jnp.zeros((4, w.shape[1]), F32)
    parts = []
    for _ in range(3):
        low = w.astype(BF16).astype(F32)
        parts += [low, pad]
        w = w - low
    return jnp.concatenate(parts, 0).astype(BF16)


def mix_of(cur, left, mo, mb):
    wide = cur.astype(F32)
    inv = lax.rsqrt(jnp.mean(wide * wide, -1, keepdims=True) + 1e-06)
    pre = lax.dot_general(cur, left, ROWS_COLS, preferred_element_type=F32)
    pre = inv * (pre[:, 0:36] + pre[:, 40:76] + pre[:, 80:116])
    hid, slope = gelu_parts(pre)
    mw = jnp.dot(hid, mo, precision=HIGH, preferred_element_type=F32) + mb
    return inv, hid, slope, mw


def blend(hist_ref, mw, wide_ref, stream_ref, rows, start=0):
    for k in range(MIXH):
        wide_ref[k] = jnp.broadcast_to(mw[:, k : k + 1], (rows, 128))
    span = 256

    for g in range(rows // 16):
        at_rows = slice(g * 16, (g + 1) * 16)

        def body(k, carry):
            at = pl.multiple_of(k * span, span)
            acc = [None] * STREAMS
            for j in range(HIST):
                h = hist_ref[j, pl.ds(start + g * 16, 16), pl.ds(at, span)].astype(F32)
                for c in range(STREAMS):
                    w = wide_ref[c * HIST + j, at_rows]
                    term = h * jnp.concatenate([w] * (span // 128), axis=1)
                    acc[c] = term if j == 0 else acc[c] + term
            for c in range(STREAMS):
                stream_ref[c, at_rows, pl.ds(at, span)] = acc[c]
            return carry

        lax.fori_loop(0, D // span, body, 0, unroll=2)


def front_kernel(
    length, history, cot, mg_in, mi_in, mo_in, mb_in, ng_in, nb_in,
    normed, resid, rows_out, own, send, total,
    hist, mg, mi, mo, mb, ng, nb, left, wide, stream, sems, big_sems,
):
    rows = QUARTER
    small = [
        pltpu.make_async_copy(src, dst, sems.at[n])
        for n, (src, dst) in enumerate(
            ((mg_in, mg), (mi_in, mi), (mo_in, mo), (mb_in, mb), (ng_in, ng), (nb_in, nb))
        )
    ]
    big = [
        pltpu.make_async_copy(
            history.at[:, pl.ds(n * rows, rows), :],
            hist.at[:, pl.ds(n * rows, rows), :],
            big_sems.at[n],
        )
        for n in range(SEQ // rows)
    ]
    for copy in small + big:
        copy.start()
    rows_kernel(length, cot, rows_out, own, send, total)
    for copy in small:
        copy.wait()
    left[...] = split_in_three(mi[...] * mg[...])
    for n in range(SEQ // rows):
        big[n].wait()
        at = slice(n * rows, (n + 1) * rows)
        _, _, _, mw = mix_of(hist[HIST - 1, at], left[...], mo[...], mb[...])
        blend(hist, mw, wide, stream, rows, n * rows)
        for c in range(STREAMS):
            s = stream[c]
            cen = s - jnp.mean(s, -1, keepdims=True)
            var = jnp.mean(cen * cen, -1, keepdims=True)
            normed[c, at] = (
                cen * lax.rsqrt(var + 1e-05) * ng[c : c + 1] + nb[c : c + 1]
            ).astype(BF16)
        resid[at] = stream[STREAMS - 1]


def front(lengths, history, cotangent, mg, mi, mo, mb, ng, nb):
    return call(
        "front",
        front_kernel,
        [SMEM, HBM, VMEM] + [HBM] * 6,
        [
            shaped((STREAMS, SEQ, D), BF16),
            shaped((SEQ, D)),
            shaped((SEQ, D), BF16),
            shaped((1024, SEQ)),
            shaped((1024, SEQ)),
            shaped((1, D)),
        ],
        (lengths, held(history), cotangent, *map(held, (mg, mi, mo, mb, ng, nb))),
        (),
        [
            pltpu.VMEM((HIST, SEQ, D), BF16),
            pltpu.VMEM((1, D), F32),
            pltpu.VMEM((MIXH, D), F32),
            pltpu.VMEM((MIXH, MIXH), F32),
            pltpu.VMEM((1, MIXH), F32),
            pltpu.VMEM((STREAMS, D), F32),
            pltpu.VMEM((STREAMS, D), F32),
            pltpu.VMEM((120, D), BF16),
            pltpu.VMEM((MIXH, QUARTER, 128), F32),
            pltpu.VMEM((STREAMS, QUARTER, D), F32),
            pltpu.SemaphoreType.DMA((6,)),
            pltpu.SemaphoreType.DMA((4,)),
        ],
        mib=24,
    )


def slot(r, h):
    first = jnp.where(r == 0, 6, jnp.where(r == 1, 4, jnp.where(r == 2, 0, 3)))
    second = jnp.where(r == 0, 7, jnp.where(r == 1, 1, jnp.where(r == 2, 2, 5)))
    return jnp.where(h == 0, first, second)


def pick(c):
    row = lax.broadcasted_iota(jnp.int32, (128, 256), 0)
    col = lax.broadcasted_iota(jnp.int32, (128, 256), 1)
    return (col == (row // 64) * 128 + c * 64 + row % 64).astype(F32).astype(BF16)


def arrange(read, own, send):
    y0, z0, c0, _ = place()
    for c, out in ((c0, own), (1 - c0, send)):
        chosen = pick(c)
        for b in range(8):
            flipped = lax.dot_general(chosen, read(b), ROWS_COLS, preferred_element_type=F32)
            for part in range(4):
                y, z, h = b // 2, (b % 2) * 2 + part // 2, part % 2
                dy, dz = (y - y0 + 4) % 4, (z - z0 + 4) % 4
                r1, r2 = jnp.where(c == 0, dy, dz), jnp.where(c == 0, dz, dy)
                inner = slot(r2, h)
                at = pl.multiple_of((slot(r1, inner // 4) * 4 + inner % 4) * 32, 32)
                out[pl.ds(at, 32), :] = flipped[part * 32 : (part + 1) * 32]


def rows_kernel(length, cot, rows_out, own, send, total):
    at = lax.broadcasted_iota(jnp.int32, (SEQ, 1), 0)
    for k in range(8):
        cols = slice(k * 256, (k + 1) * 256)
        g = jnp.where(at < length[0], cot[:, cols].astype(F32), 0.0)
        rows_out[:, cols] = g.astype(BF16)
        total[:, cols] = jnp.sum(g, 0, keepdims=True)
    arrange(lambda b: rows_out[:, b * 256 : (b + 1) * 256], own, send)


def pack(rows, out, part):
    for k in range(4):
        out[part + k // 2, :, (k % 2) * 256 : (k % 2 + 1) * 256] = rows[k * 256 : (k + 1) * 256]


def unpack(box, part):
    pieces = [
        box[part + k // 2, :, (k % 2) * 256 : (k % 2 + 1) * 256].astype(BF16) for k in range(4)
    ]
    return jnp.concatenate(pieces, 0)


def normed_kernel(x, own, send):
    for s in range(3):
        arrange(lambda b: x[s, :, b * 256 : (b + 1) * 256], own.at[s], send.at[s])


def normed_arranged(normed, after=()):
    return call(
        "normed_arranged",
        normed_kernel,
        [VMEM],
        [shaped((3, 1024, SEQ))] * 2,
        (normed,),
        after,
    )


def fc1_kernel(x, w, b, g_send, box, slope):
    for j in range(4):
        cols = slice(j * 512, (j + 1) * 512)
        pre = jnp.dot(x[3], w[:, cols], preferred_element_type=F32) + b[:, cols]
        value, grad = gelu_parts(pre)
        box[j] = rounded(value)
        slope[j] = grad
    pack(g_send, box, 4)


def fc1(normed, w_fc1, b_fc1, g_send, after=()):
    return call(
        "fc1",
        fc1_kernel,
        [VMEM] * 4,
        [shaped((6, SEQ, 512)), shaped((4, SEQ, 512))],
        (normed, w_fc1, b_fc1, g_send),
        after,
    )


def hidden_kernel(g, w, slope, normed, box, total, own, send):
    for j in range(4):
        cols = slice(j * 512, (j + 1) * 512)
        grad = lax.dot_general(g[...], w[cols, :], ROWS_COLS, preferred_element_type=F32)
        low = rounded(grad * slope[j])
        box[j] = low
        total[:, cols] = jnp.sum(low, 0, keepdims=True)
    arrange(lambda b: normed[3, :, b * 256 : (b + 1) * 256], own, send)
    pack(send, box, 4)


def grad_hidden_of(rows, w_fc2, slope, normed, after=()):
    return call(
        "grad_hidden",
        hidden_kernel,
        [VMEM] * 4,
        [shaped((6, SEQ, 512)), shaped((1, D)), shaped((1024, SEQ))],
        (rows, w_fc2, slope, normed),
        after,
        [pltpu.VMEM((1024, SEQ), F32)],
    )


def in_ring_order(read):
    _, _, c, x = place()
    parts = []
    for r in (1, 2, 3, 0):
        at = pl.multiple_of(x_chunk(c, x, r) * QUARTER, QUARTER)
        parts.append(read(pl.ds(at, QUARTER)))
    return jnp.concatenate(parts, 0).astype(BF16)


def to_quarters(res, outs, part, cols):
    for k, out in enumerate(outs):
        out[part, :, cols] = res[k * QUARTER : (k + 1) * QUARTER]


def backs_kernel(
    box_a, box_b, box_c, w1_in, w_t, wo, w2_in, o1, o2, o3, o0, gh, act, w1, w2, sems
):
    outs = (o1, o2, o3, o0)
    blocks = [slice(j * 512, (j + 1) * 512) for j in range(4)]
    first = [
        pltpu.make_async_copy(w1_in.at[pl.ds(j * 512, 512), :], w1.at[j], sems.at[j])
        for j in range(4)
    ]
    last = [
        pltpu.make_async_copy(w2_in.at[:, pl.ds(j * 512, 512)], w2.at[j % 2], sems.at[4 + j])
        for j in range(4)
    ]
    for copy in first + last[:2]:
        copy.start()
    for j, cols in enumerate(blocks):
        gh[:, cols] = in_ring_order(lambda rows: box_b[j, rows, :])
        act[:, cols] = in_ring_order(lambda rows: box_a[j, rows, :])
    for c in range(3):
        lhs = in_ring_order(lambda rows: box_c[c + 1, rows, :])
        for cols in blocks:
            res = lax.dot_general(lhs, w_t[c, cols, :], ROWS_COLS, preferred_element_type=F32)
            to_quarters(res, outs, c, cols)
    for j, cols in enumerate(blocks):
        first[j].wait()
        res = lax.dot_general(gh[...], w1[j], ROWS_COLS, preferred_element_type=F32)
        to_quarters(res, outs, 3, cols)
    lhs = in_ring_order(lambda rows: box_c[0, rows, :])
    for j, cols in enumerate(blocks):
        last[j].wait()
        res = jnp.dot(lhs, wo[:, cols], preferred_element_type=F32)
        res = res + jnp.dot(act[...], w2[j % 2], preferred_element_type=F32)
        to_quarters(res, outs, 4, cols)
        if j < 2:
            last[j + 2].start()


def backs(box_a, box_b, box_c, w_fc1, w_t, w_out, w_fc2, after=()):
    return call(
        "backs",
        backs_kernel,
        [VMEM] * 3 + [HBM, VMEM, VMEM, HBM],
        [shaped((5, QUARTER, D))] * 4,
        (box_a, box_b, box_c, held(w_fc1), w_t, w_out, held(w_fc2)),
        after,
        [
            pltpu.VMEM((SEQ, D), BF16),
            pltpu.VMEM((SEQ, D), BF16),
            pltpu.VMEM((4, 512, D), BF16),
            pltpu.VMEM((2, D, 512), BF16),
            pltpu.SemaphoreType.DMA((8,)),
        ],
        mib=20,
    )


def turn(v, cos, lead, tail, sign):
    return v * cos + sign * (pltpu.roll(v, HD - 16, 1) * lead + pltpu.roll(v, 16, 1) * tail)


def attn_kernel(length, normed, w, b, rows, wo, send, cos_ref, lead_ref, tail_ref, mid, total):
    for c in range(3):
        pack(send.at[c], mid, 4 + 2 * c)
    scale = 1.0 / math.sqrt(HD)
    cos, lead, tail = cos_ref[...], lead_ref[...], tail_ref[...]
    at_q = lax.broadcasted_iota(jnp.int32, (SEQ, SEQ), 0)
    at_k = lax.broadcasted_iota(jnp.int32, (SEQ, SEQ), 1)
    allowed = (at_k <= at_q) & (at_k < length[0])
    for pair in range(2):
        wide = slice(pair * 2 * HD, (pair + 1) * 2 * HD)
        proj = [
            jnp.dot(normed[c], w[c, :, wide], preferred_element_type=F32) + b[c : c + 1, wide]
            for c in range(3)
        ]
        grad_ctx = lax.dot_general(rows[...], wo[wide, :], ROWS_COLS, preferred_element_type=F32)
        for n in range(2):
            cols = slice(n * HD, (n + 1) * HD)
            to = slice((pair * 2 + n) * HD, (pair * 2 + n + 1) * HD)
            q = turn(proj[0][:, cols], cos, lead, tail, 1.0).astype(BF16)
            k = turn(proj[1][:, cols], cos, lead, tail, 1.0).astype(BF16)
            v = proj[2][:, cols].astype(BF16)
            gc = grad_ctx[:, cols].astype(BF16)
            scores = lax.dot_general(q, k, ROWS_COLS, preferred_element_type=F32) * scale
            scores = jnp.where(allowed, scores, -1e30)
            weights = jnp.exp(scores - jnp.max(scores, -1, keepdims=True))
            probs = weights / jnp.sum(weights, -1, keepdims=True)
            low = probs.astype(BF16)
            mid[0, :, to] = rounded(jnp.dot(low, v, preferred_element_type=F32))
            gp = lax.dot_general(gc, v, ROWS_COLS, preferred_element_type=F32)
            gs = (probs * (gp - jnp.sum(probs * gp, -1, keepdims=True))).astype(BF16)
            gv = lax.dot_general(low, gc, ROWS_ROWS, preferred_element_type=F32)
            gq = jnp.dot(gs, k, preferred_element_type=F32) * scale
            gk = lax.dot_general(gs, q, ROWS_ROWS, preferred_element_type=F32) * scale
            grads = (turn(gq, cos, lead, tail, -1.0), turn(gk, cos, lead, tail, -1.0), gv)
            for c in range(3):
                g = rounded(grads[c])
                mid[c + 1, :, to] = g
                total[c : c + 1, to] = jnp.sum(g, 0, keepdims=True)


def rotary():
    half = ROT // 2
    position = np.arange(SEQ, dtype=np.float32)
    freq_steps = np.arange(0, ROT, 2, dtype=np.float32) / np.float32(ROT)
    inverse = np.exp(freq_steps * np.float32(-math.log(10000.0)))
    angles = position[:, None] * inverse[None, :]
    cos, sin = np.cos(angles), np.sin(angles)
    wide = np.ones((SEQ, HD), np.float32)
    lead, tail = np.zeros((SEQ, HD), np.float32), np.zeros((SEQ, HD), np.float32)
    wide[:, :half], wide[:, half:ROT] = cos, cos
    lead[:, :half], tail[:, half:ROT] = -sin, sin
    return jnp.asarray(wide), jnp.asarray(lead), jnp.asarray(tail)


def attention(lengths, normed, w_t, b_qkv, rows, w_out, send, tables, after=()):
    return call(
        "attention",
        attn_kernel,
        [SMEM] + [VMEM] * 9,
        [shaped((10, SEQ, 512)), shaped((3, 512))],
        (lengths, normed, w_t, b_qkv, rows, w_out, send, *tables),
        after,
    )


def wgrad_kernel(which, n_own, *refs):
    owns, boxes = refs[:n_own], refs[n_own:-4]
    box, up, down, rest = refs[-4:]
    mate = boxes[0]
    made = None
    for j in range(4):
        cols = slice(j * 512, (j + 1) * 512)
        if j == 0 or which[j] != which[j - 1]:
            n, k, m, part = which[j]
            own = owns[n][...] if k is None else owns[n][k]
            made = jnp.concatenate([own.astype(BF16), unpack(boxes[m], part)], 1)
        right = jnp.concatenate([box[j].astype(BF16), mate[j].astype(BF16)], 0)
        res = jnp.dot(made, right, preferred_element_type=F32)
        up[:, cols] = res[:256]
        down[:, cols] = res[256:512]
        rest[:, cols] = res[512:]


def wgrad(name, owns, boxes, which, box, after=()):
    args = list(owns) + list(boxes) + [box]
    return call(
        name,
        functools.partial(wgrad_kernel, which, len(owns)),
        [VMEM] * len(args),
        [shaped((256, D)), shaped((256, D)), shaped((512, D))],
        args,
        after,
    )


def relay_kernel(rest, up1, down1, up, down):
    up[...] = rest[:128] + up1[:128]
    down[...] = rest[128:256] + down1[:128]


def relay(name, rest, one, after=()):
    return call(
        name,
        relay_kernel,
        [VMEM] * 3,
        [shaped((128, D))] * 2,
        (rest, *one),
        after,
    )


def cross_kernel(*refs):
    *ins, up, down, kept = refs
    for n in range(3):
        rest, up1, down1, up2, down2 = ins[5 * n : 5 * n + 5]
        cols = slice(n * D, (n + 1) * D)
        head = rest[256:384] + down1[128:] + up2[...]
        up[:, cols] = head[:64]
        down[:, cols] = head[64:]
        kept[:, cols] = rest[384:] + up1[128:] + down2[...]


def cross(pieces, after=()):
    args = [a for piece in pieces for a in piece]
    return call(
        "cross",
        cross_kernel,
        [VMEM] * len(args),
        [shaped((64, 3 * D)), shaped((64, 3 * D)), shaped((128, 3 * D))],
        args,
        after,
    )


def second_kernel(kept, got_up, got_down, up, down):
    up[...] = kept[:32] + got_up[:32]
    down[...] = kept[32:64] + got_down[:32]


def second(kept, got_up, got_down, after=()):
    return call(
        "second",
        second_kernel,
        [VMEM] * 3,
        [shaped((32, 3 * D))] * 2,
        (kept, got_up, got_down),
        after,
    )


def third_kernel(kept, got_up, got_down, last_up, last_down, fc2, fc1, out, qkv):
    homes = [(fc2, 0, D), (fc1, D, D), (out, 2 * D, 512)]
    homes += [(qkv.at[c], 2 * D + 512 * (c + 1), 512) for c in range(3)]
    for home, at, width in homes:
        cols = slice(at, at + width)
        home[:32] = kept[64:96, cols] + got_down[32:, cols] + last_up[:, cols]
        home[32:] = kept[96:, cols] + got_up[32:, cols] + last_down[:, cols]


def third(kept, got_up, got_down, last_up, last_down, after=()):
    return call(
        "third",
        third_kernel,
        [VMEM] * 5,
        [shaped((64, D)), shaped((64, D)), shaped((64, 512)), shaped((3, 64, 512))],
        (kept, got_up, got_down, last_up, last_down),
        after,
    )


def back_kernel(
    hist, cot, mine, others, mg_ref, mi_ref, mo_ref, mb_ref, ng_ref,
    grad_hist, sums, small, left, wide, stream, product,
):
    rows = hist.shape[1]
    mg, mi, mo = mg_ref[...], mi_ref[...], mo_ref[...]
    sums[...] = jnp.zeros_like(sums)
    small[...] = jnp.zeros_like(small)
    left[...] = split_in_three(mi * mg)

    inv, hid, slope, mw = mix_of(hist[HIST - 1], left[...], mo, mb_ref[...])
    blend(hist, mw, wide, stream, rows)
    for c in range(STREAMS):
        g = mine[c] + others[c]
        s = stream[c]
        cen = s - jnp.mean(s, -1, keepdims=True)
        rstd = lax.rsqrt(jnp.mean(cen * cen, -1, keepdims=True) + 1e-05)
        hat = cen * rstd
        sums[36 + c : 37 + c, :] += jnp.sum(g * hat, 0, keepdims=True)
        sums[40 + c : 41 + c, :] += jnp.sum(g, 0, keepdims=True)
        gh = g * ng_ref[c : c + 1]
        ds = rstd * (
            gh - jnp.mean(gh, -1, keepdims=True) - hat * jnp.mean(gh * hat, -1, keepdims=True)
        )
        if c == 3:
            ds = ds + cot[...].astype(F32)
        stream[c] = ds
    for g in range(rows // 16):
        at_rows = slice(g * 16, (g + 1) * 16)
        for c in range(STREAMS):
            for j in range(HIST):
                acc = None
                for k in range(D // 256):
                    cols = slice(k * 256, (k + 1) * 256)
                    term = stream[c, at_rows, cols] * hist[j, at_rows, cols].astype(F32)
                    acc = term if acc is None else acc + term
                product[c * HIST + j, at_rows] = acc[:, :128] + acc[:, 128:]
    lane = lax.broadcasted_iota(jnp.int32, (rows, MIXH), 1)
    gm = jnp.zeros((rows, MIXH), F32)
    for k in range(MIXH):
        gm = jnp.where(lane == k, jnp.sum(product[k], -1, keepdims=True), gm)
    small[36:37, :MIXH] += jnp.sum(gm, 0, keepdims=True)
    small[:MIXH, :MIXH] += lax.dot_general(
        hid, gm, ROWS_ROWS, precision=HIGH, preferred_element_type=F32
    )
    d_pre = slope * lax.dot_general(
        gm, mo, ROWS_COLS, precision=HIGH, preferred_element_type=F32
    )
    low = (inv * d_pre).T
    pad = jnp.zeros((4, rows), F32)
    parts = []
    for _ in range(3):
        part = low.astype(BF16).astype(F32)
        parts += [part, pad]
        low = low - part
    turned_pre = jnp.concatenate(parts, 0).astype(BF16)
    cur_low = hist[HIST - 1]
    three = jnp.dot(turned_pre, cur_low, preferred_element_type=F32)
    outer = three[0:36] + three[40:76] + three[80:116]
    sums[:MIXH, :] += outer * mg
    sums[44:45, :] += jnp.sum(outer * mi, 0, keepdims=True)
    d_unit = jnp.dot(d_pre, mi * mg, precision=HIGH, preferred_element_type=F32)
    unit = cur_low.astype(F32) * inv
    d_cur = inv * (d_unit - unit * jnp.mean(d_unit * unit, -1, keepdims=True))
    span = 256
    for g in range(rows // 16):
        at_rows = slice(g * 16, (g + 1) * 16)
        for k in range(D // span):
            cols = slice(k * span, (k + 1) * span)
            ds = [stream[c, at_rows, cols] for c in range(STREAMS)]
            for j in range(HIST):
                acc = d_cur[at_rows, cols] if j == HIST - 1 else None
                for c in range(STREAMS):
                    w = wide[c * HIST + j, at_rows]
                    term = ds[c] * jnp.concatenate([w] * (span // 128), axis=1)
                    acc = term if acc is None else acc + term
                grad_hist[j, at_rows, cols] = acc.astype(BF16)


def front_back(history, cotangent, mine, others, mg, mi, mo, mb, ng, after=()):
    rows = QUARTER
    x = lax.axis_index("tensor")
    hist = lax.dynamic_slice_in_dim(history, x * QUARTER, QUARTER, 1)
    cot = lax.dynamic_slice_in_dim(cotangent, x * QUARTER, QUARTER, 0)
    return call(
        "front_back",
        back_kernel,
        [VMEM] * 9,
        [shaped((HIST, QUARTER, D), BF16), shaped((48, D)), shaped((40, 128))],
        (hist, cot, mine, others, mg, mi, mo, mb, ng),
        after,
        [
            pltpu.VMEM((120, D), BF16),
            pltpu.VMEM((MIXH, rows, 128), F32),
            pltpu.VMEM((STREAMS, rows, D), F32),
            pltpu.VMEM((MIXH, rows, 128), F32),
        ],
    )


def out_kernel(info, own, part, resid, bias, out):
    start = pl.multiple_of(info[0] * QUARTER, QUARTER)
    at = lax.broadcasted_iota(jnp.int32, (QUARTER, 1), 0) + start
    valid = jnp.where(at < info[1], 1.0, 0.0)
    rows = resid[pl.ds(start, QUARTER), :]
    out[...] = rounded(rows + valid * (own[4] + part[4] + bias[...]))


def out_rows(info, own, part, resid, bias, after=()):
    return call(
        "out_rows",
        out_kernel,
        [SMEM] + [VMEM] * 4,
        shaped((QUARTER, D)),
        (info, own, part, resid, bias),
        after,
    )


def gather_kernel(r1, r2, r3, r0, out):
    _, _, c, x = place()
    for r, ref in ((1, r1), (2, r2), (3, r3), (0, r0)):
        at = pl.multiple_of(x_chunk(c, x, r) * QUARTER, QUARTER)
        out[pl.ds(at, QUARTER), :] = ref[...].astype(BF16)


def gathered(parts, after=()):
    return call("gathered", gather_kernel, [VMEM] * 4, shaped((SEQ, D), BF16), parts, after)


def add_kernel(a, b, out):
    out[...] = a[...] + b[...]


def plus(name, a, b, after=()):
    return call(name, add_kernel, [VMEM] * 2, shaped(a.shape), (a, b), after)


def as_tiles(a):
    rows, cols = a.shape
    return a.reshape(rows // 8, 8, cols // 128, 128).transpose(0, 2, 1, 3).reshape(-1, 8, 128)


def from_tiles(tiles, rows, cols):
    return tiles.reshape(rows // 8, cols // 128, 8, 128).transpose(0, 2, 1, 3).reshape(rows, cols)


def sum_all(tiles):
    each = lax.all_to_all(tiles, ALL, 0, 0, tiled=True)
    mine = jnp.sum(each, 0, keepdims=True)
    return lax.all_to_all(jnp.broadcast_to(mine, tiles.shape), ALL, 0, 0, tiled=True)


def local(
    history, lengths, cotangent, w_qkv, b_qkv, w_out, w_fc1, b_fc1, w_fc2, out_bias,
    norm_gain, norm_bias, mix_gain, mix_in, mix_out, mix_bias,
):
    x = lax.axis_index("tensor")
    mg, mi, mb = mix_gain[None], mix_in.T, mix_bias[None]
    w_t = w_qkv.transpose(1, 0, 2)

    normed, resid, rows, g_own, g_send, sum_rows = front(
        lengths, history, cotangent, mg, mi, mix_out, mb, norm_gain, norm_bias
    )
    box_a, slope = fc1(normed, w_fc1, b_fc1[None], g_send)
    mate_a = to_mate(box_a)
    box_b, sum_hidden, n3_own = grad_hidden_of(rows, w_fc2, slope, normed)
    mate_b = to_mate(box_b)
    n_own, n_send = normed_arranged(normed, (n3_own,))
    up, down, rest_a = wgrad("wgrad_a", (g_own,), (mate_a,), ((0, None, 0, 4),) * 4, box_a, (n_own,))
    a1 = to_yz(up, 1, 0), to_yz(down, -1, 0)
    box_c, sum_proj = attention(
        lengths, normed, w_t, b_qkv, rows, w_out, n_send, rotary(), (up,)
    )
    mate_c = to_mate(box_c)
    five = backs(box_a, box_b, box_c, w_fc1, w_t, w_out, w_fc2)
    others = to_x(five[0])
    up, down, rest_b = wgrad(
        "wgrad_b", (n3_own,), (mate_b,), ((0, None, 0, 4),) * 4, box_b, (five[0],)
    )
    b1 = to_yz(up, 1, 0), to_yz(down, -1, 0)
    up, down = relay("relay_a", rest_a, a1, (up,))
    a2 = to_yz(up, 1, 0), to_yz(down, -1, 0)
    which = ((0, None, 1, 4), (1, 0, 0, 4), (1, 1, 0, 6), (1, 2, 0, 8))
    up, down, rest_c = wgrad("wgrad_c", (g_own, n_own), (mate_c, mate_a), which, box_c, (up,))
    c1 = to_yz(up, 1, 0), to_yz(down, -1, 0)
    step = plus("plus_1", five[1], others, (up,))
    others = to_x(step)
    up, down = relay("relay_b", rest_b, b1, (step,))
    b2 = to_yz(up, 1, 0), to_yz(down, -1, 0)
    step = plus("plus_2", five[2], others, (up,))
    others = to_x(step)
    up, down = relay("relay_c", rest_c, c1, (step,))
    c2 = to_yz(up, 1, 0), to_yz(down, -1, 0)
    pieces = ((rest_a, *a1, *a2), (rest_b, *b1, *b2), (rest_c, *c1, *c2))
    up, down, kept = cross(pieces, (up,))
    n1 = to_yz(up, 1, 1), to_yz(down, -1, 1)

    info = jnp.stack([x, lengths[0]])
    mine = out_rows(info, five[3], others, resid, out_bias[None], (up,))
    got1 = to_x(mine)
    grad_history, sums, small = front_back(
        history, cotangent, five[3], others, mg, mi, mix_out, mb, norm_gain, (mine,)
    )
    up, down = second(kept, *n1, (small,))
    n2 = to_yz(up, 1, 1), to_yz(down, -1, 1)
    got2 = to_x(got1)
    got3 = to_x(got2)
    grad_fc2, grad_fc1, grad_out, grad_qkv = third(kept, *n1, *n2)
    block_out = gathered((got1, got2, got3, mine))

    zero = jnp.int32(0)
    early = jnp.zeros((8, D), F32)
    early = lax.dynamic_update_slice(early, sum_hidden, (x, zero))
    early = lax.dynamic_update_slice(early, sum_proj, (jnp.int32(4), x * 512))
    early = lax.dynamic_update_slice(
        early, jnp.where(x == 0, sum_rows, 0.0), (jnp.int32(7), zero)
    )
    tiles = jnp.concatenate(
        [as_tiles(sums), as_tiles(early), as_tiles(small), jnp.zeros((11, 8, 128), F32)], 0
    )
    total = sum_all(tiles)
    sums = from_tiles(total[:96], 48, D)
    early = from_tiles(total[96:112], 8, D)
    small = total[112:117].reshape(40, 128)

    return (
        block_out,
        grad_history,
        grad_qkv.transpose(1, 0, 2),
        early[4:7],
        grad_out.T,
        grad_fc1,
        early[:4].reshape(-1),
        grad_fc2.T,
        early[7],
        sums[36:40],
        sums[40:44],
        sums[44],
        sums[:MIXH].T,
        small[:MIXH, :MIXH],
        small[MIXH, :MIXH],
    )


def solution(mesh):
    in_specs = (
        P(None, "dp", None),
        P("dp"),
        P("dp", None),
        P(None, None, "tensor"),
        P(None, "tensor"),
        P("tensor", None),
        P(None, "tensor"),
        P("tensor"),
        P("tensor", None),
        P(),
        P(),
        P(),
        P(),
        P(),
        P(),
        P(),
    )
    out_specs = (
        P("dp", None),
        P(None, ("dp", "tensor"), None),
        P("dp", None, "tensor"),
        P(),
        P("tensor", "dp"),
        P("dp", "tensor"),
        P(),
        P("tensor", "dp"),
        P(),
        P(),
        P(),
        P(),
        P(),
        P(),
        P(),
    )
    return jax.shard_map(local, mesh=mesh, in_specs=in_specs, out_specs=out_specs, check_vma=False)
```

```python
import functools
import math

import jax
import jax.numpy as jnp
import numpy as np
from jax import lax
from jax.experimental import pallas as pl
from jax.experimental.pallas import tpu as pltpu
from jax.sharding import PartitionSpec as P

D = 2048
HD = 128
ROT = 32
HIST = 9
STREAMS = 4
MIXH = 36
SEQ = 256
QUARTER = 64
F32 = jnp.float32
BF16 = jnp.bfloat16
HIGH = lax.Precision.HIGHEST
ROWS_COLS = (((1,), (1,)), ((), ()))
ROWS_ROWS = (((0,), (0,)), ((), ()))
ALL = ("dp", "tensor")


def place():
    dp = lax.axis_index("dp")
    return dp // 8, (dp // 2) % 4, dp % 2, lax.axis_index("tensor")


def dp_of(y, z, c):
    return ((y % 4) * 4 + z % 4) * 2 + c


def yz_pairs(step, phase):
    out = []
    for y in range(4):
        for z in range(4):
            for c in range(2):
                along_y = c == phase
                to = dp_of(y + step, z, c) if along_y else dp_of(y, z + step, c)
                out.append((dp_of(y, z, c), to))
    return out


def x_pairs():
    out = []
    for d in range(32):
        for x in range(4):
            out.append((d * 4 + x, d * 4 + (x + (1 if d % 2 == 0 else 3)) % 4))
    return out


def to_yz(a, step, phase):
    return lax.ppermute(a, "dp", yz_pairs(step, phase))


def to_x(a):
    return lax.ppermute(a, ALL, x_pairs())


def to_mate(a):
    return lax.ppermute(a, "dp", [(d, d ^ 1) for d in range(32)])


def x_chunk(c, x, r):
    return jnp.where(c == 0, x - r + 4, x + r) % 4


def gelu_parts(v):
    cdf = 0.5 * (1.0 + lax.erf(v * math.sqrt(0.5)))
    pdf = jnp.exp(-0.5 * v * v) * (1.0 / math.sqrt(2.0 * math.pi))
    return v * cdf, cdf + v * pdf


def rounded(v):
    return v.astype(BF16).astype(F32)


VMEM = pl.BlockSpec(memory_space=pltpu.VMEM)
SMEM = pl.BlockSpec(memory_space=pltpu.SMEM)
ANY = pl.BlockSpec(memory_space=pl.ANY)
HBM = pl.BlockSpec(memory_space=pltpu.HBM)


COST = {
    "wgrad_a": 0.1,
    "ffn_back": 0.5,
    "plus_1": 2.0,
    "branches": 6.0,
    "wgrad_c": 1.0,
    "plus_2": 0.5,
    "relay_ab": 2.0,
    "plus_3": 2.0,
    "relay_c": 2.0,
    "cross_ab": 10.0,
    "cross_c": 10.0,
    "open": 30.0,
}


def call(name, kernel, in_specs, out_shape, args, after=(), scratch=(), grid=(), out_specs=None, mib=16, aliases=None):
    n_in, n_after = len(in_specs), len(after)

    def body(*refs):
        kernel(*refs[:n_in], *refs[n_in + n_after :])

    if out_specs is None:
        out_specs = jax.tree.map(lambda _: VMEM, out_shape)
    return pl.pallas_call(
        body,
        name=name,
        grid=grid,
        in_specs=list(in_specs) + [ANY] * n_after,
        out_specs=out_specs,
        scratch_shapes=list(scratch),
        out_shape=out_shape,
        input_output_aliases=aliases or {},
        compiler_params=pltpu.CompilerParams(vmem_limit_bytes=mib * 1024 * 1024),
        cost_estimate=pl.CostEstimate(
            flops=int(COST.get(name, 0.01) * 1e9), bytes_accessed=1, transcendentals=0
        ),
    )(*args, *after)


def held(a):
    return pltpu.with_memory_space_constraint(a, pltpu.HBM)


def whole(shape):
    return pl.BlockSpec(shape, lambda *_: (0,) * len(shape))


def shaped(shape, dtype=F32):
    return jax.ShapeDtypeStruct(shape, dtype)


def split_in_three(w):
    pad = jnp.zeros((4, w.shape[1]), F32)
    parts = []
    for _ in range(3):
        low = w.astype(BF16).astype(F32)
        parts += [low, pad]
        w = w - low
    return jnp.concatenate(parts, 0).astype(BF16)


def mix_of(cur, left, mo, mb):
    wide = cur.astype(F32)
    inv = lax.rsqrt(jnp.mean(wide * wide, -1, keepdims=True) + 1e-06)
    pre = lax.dot_general(cur, left, ROWS_COLS, preferred_element_type=F32)
    pre = inv * (pre[:, 0:36] + pre[:, 40:76] + pre[:, 80:116])
    hid, slope = gelu_parts(pre)
    mw = jnp.dot(hid, mo, precision=HIGH, preferred_element_type=F32) + mb
    return inv, hid, slope, mw


SPREAD = 256


def spreading():
    row = lax.broadcasted_iota(jnp.int32, (MIXH, STREAMS * SPREAD), 0)
    col = lax.broadcasted_iota(jnp.int32, (MIXH, STREAMS * SPREAD), 1)
    at = col % SPREAD
    hit = (row == (col // SPREAD) * HIST + at // 16) & (at < HIST * 16)
    return hit.astype(F32).astype(BF16)


def block_diagonal(mw, spread):
    rows = mw.shape[0]
    row = lax.broadcasted_iota(jnp.int32, (rows, STREAMS * SPREAD), 0)
    col = lax.broadcasted_iota(jnp.int32, (rows, STREAMS * SPREAD), 1)
    same = row % 16 == col % 16
    high = mw.astype(BF16)
    low = (mw - high.astype(F32)).astype(BF16)
    out = []
    for part in (high, low):
        wide = jnp.dot(part, spread, preferred_element_type=F32)
        out.append(jnp.where(same, wide, 0.0).astype(BF16))
    return out


def blend(hist_ref, blocks, stream_ref, rows, start=0):
    totals = []
    for g in range(rows // 16):
        at = slice(g * 16, (g + 1) * 16)
        left = jnp.concatenate(
            [
                part[at, c * SPREAD : c * SPREAD + HIST * 16]
                for part in blocks
                for c in range(STREAMS)
            ],
            0,
        )
        total = None
        for k in range(D // 256):
            cols = slice(k * 256, (k + 1) * 256)
            right = jnp.concatenate(
                [hist_ref[j, pl.ds(start + g * 16, 16), cols] for j in range(HIST)], 0
            )
            res = jnp.dot(left, right, preferred_element_type=F32)
            res = res[: STREAMS * 16] + res[STREAMS * 16 :]
            for c in range(STREAMS):
                stream_ref[c, at, cols] = res[c * 16 : (c + 1) * 16]
            part = res[:, :128] + res[:, 128:]
            total = part if total is None else total + part
        totals.append(jnp.sum(total, -1, keepdims=True))
    return totals


def norm_parts(stream_ref, totals, c, g):
    at = slice(g * 16, (g + 1) * 16)
    mean = totals[g][c * 16 : (c + 1) * 16] * (1.0 / D)
    total = None
    for k in range(D // 256):
        cen = stream_ref[c, at, k * 256 : (k + 1) * 256] - mean
        sq = cen * cen
        part = sq[:, :128] + sq[:, 128:]
        total = part if total is None else total + part
    var = jnp.sum(total, -1, keepdims=True) * (1.0 / D)
    return mean, lax.rsqrt(var + 1e-05)


def front_kernel(
    length, history, cot, mg_in, mi_in, mo_in, mb_in, ng_in, nb_in,
    normed, rows_out, own, send, total,
    hist, mg, mi, mo, mb, ng, nb, left, spread, stream, sems, big_sems,
):
    rows = QUARTER
    small = [
        pltpu.make_async_copy(src, dst, sems.at[n])
        for n, (src, dst) in enumerate(
            ((mg_in, mg), (mi_in, mi), (mo_in, mo), (mb_in, mb), (ng_in, ng), (nb_in, nb))
        )
    ]
    big = [
        pltpu.make_async_copy(
            history.at[:, pl.ds(n * rows, rows), :],
            hist.at[:, pl.ds(n * rows, rows), :],
            big_sems.at[n],
        )
        for n in range(SEQ // rows)
    ]
    for copy in small + big:
        copy.start()
    rows_kernel(length, cot, rows_out, own, send, total)
    for copy in small:
        copy.wait()
    left[...] = split_in_three(mi[...] * mg[...])
    spread[...] = spreading()

    def chunk(n, carry):
        start = pl.multiple_of(n * rows, rows)
        pltpu.make_async_copy(
            history.at[:, pl.ds(start, rows), :],
            hist.at[:, pl.ds(start, rows), :],
            big_sems.at[n],
        ).wait()
        _, _, _, mw = mix_of(hist[HIST - 1, pl.ds(start, rows)], left[...], mo[...], mb[...])
        totals = blend(hist, block_diagonal(mw, spread[...]), stream, rows, start)
        for g in range(rows // 16):
            at = slice(g * 16, (g + 1) * 16)
            for c in range(STREAMS):
                mean, rstd = norm_parts(stream, totals, c, g)
                for k in range(D // 512):
                    cols = slice(k * 512, (k + 1) * 512)
                    cen = stream[c, at, cols] - mean
                    normed[c, pl.ds(start + g * 16, 16), cols] = (
                        cen * rstd * ng[c : c + 1, cols] + nb[c : c + 1, cols]
                    ).astype(BF16)
        return carry

    lax.fori_loop(0, SEQ // rows, chunk, 0)


def front(lengths, history, cotangent, mg, mi, mo, mb, ng, nb):
    return call(
        "front",
        front_kernel,
        [SMEM, HBM, VMEM] + [HBM] * 6,
        [
            shaped((STREAMS, SEQ, D), BF16),
            shaped((SEQ, D), BF16),
            shaped((1024, SEQ), BF16),
            shaped((1024, SEQ)),
            shaped((1, D)),
        ],
        (lengths, held(history), cotangent, *map(held, (mg, mi, mo, mb, ng, nb))),
        (),
        [
            pltpu.VMEM((HIST, SEQ, D), BF16),
            pltpu.VMEM((1, D), F32),
            pltpu.VMEM((MIXH, D), F32),
            pltpu.VMEM((MIXH, MIXH), F32),
            pltpu.VMEM((1, MIXH), F32),
            pltpu.VMEM((STREAMS, D), F32),
            pltpu.VMEM((STREAMS, D), F32),
            pltpu.VMEM((120, D), BF16),
            pltpu.VMEM((MIXH, STREAMS * SPREAD), BF16),
            pltpu.VMEM((STREAMS, QUARTER, D), F32),
            pltpu.SemaphoreType.DMA((6,)),
            pltpu.SemaphoreType.DMA((4,)),
        ],
        mib=24,
    )


def slot(r, h):
    first = jnp.where(r == 0, 6, jnp.where(r == 1, 4, jnp.where(r == 2, 0, 3)))
    second = jnp.where(r == 0, 7, jnp.where(r == 1, 1, jnp.where(r == 2, 2, 5)))
    return jnp.where(h == 0, first, second)


def pick(c):
    row = lax.broadcasted_iota(jnp.int32, (128, 256), 0)
    col = lax.broadcasted_iota(jnp.int32, (128, 256), 1)
    return (col == (row // 64) * 128 + c * 64 + row % 64).astype(F32).astype(BF16)


def arrange(read, own, send):
    y0, z0, c0, _ = place()
    for c, out in ((c0, own), (1 - c0, send)):
        chosen = pick(c)
        for b in range(8):
            flipped = lax.dot_general(chosen, read(b), ROWS_COLS, preferred_element_type=F32)
            for part in range(4):
                y, z, h = b // 2, (b % 2) * 2 + part // 2, part % 2
                dy, dz = (y - y0 + 4) % 4, (z - z0 + 4) % 4
                r1, r2 = jnp.where(c == 0, dy, dz), jnp.where(c == 0, dz, dy)
                inner = slot(r2, h)
                at = pl.multiple_of((slot(r1, inner // 4) * 4 + inner % 4) * 32, 32)
                out[pl.ds(at, 32), :] = flipped[part * 32 : (part + 1) * 32].astype(out.dtype)


def rows_kernel(length, cot, rows_out, own, send, total):
    at = lax.broadcasted_iota(jnp.int32, (SEQ, 1), 0)
    for k in range(8):
        cols = slice(k * 256, (k + 1) * 256)
        g = jnp.where(at < length[0], cot[:, cols].astype(F32), 0.0)
        rows_out[:, cols] = g.astype(BF16)
        total[:, cols] = jnp.sum(g, 0, keepdims=True)
    arrange(lambda b: rows_out[:, b * 256 : (b + 1) * 256], own, send)


def pack(rows, first, second):
    for k in range(4):
        out = first if k < 2 else second
        out[:, (k % 2) * 256 : (k % 2 + 1) * 256] = rows[k * 256 : (k + 1) * 256]


def unpack(first, second):
    pieces = [
        out[:, k * 256 : (k + 1) * 256].astype(BF16) for out in (first, second) for k in range(2)
    ]
    return jnp.concatenate(pieces, 0)


def fc1_kernel(x, w, b, g_send, box, slope):
    for j in range(4):
        cols = slice(j * 512, (j + 1) * 512)
        pre = jnp.dot(x[3], w[:, cols], preferred_element_type=F32) + b[:, cols]
        value, grad = gelu_parts(pre)
        box[j] = rounded(value)
        slope[j] = grad
    pack(g_send, box.at[4], box.at[5])


def fc1(normed, w_fc1, b_fc1, g_send, after=()):
    return call(
        "fc1",
        fc1_kernel,
        [VMEM] * 4,
        [shaped((6, SEQ, 512)), shaped((4, SEQ, 512))],
        (normed, w_fc1, b_fc1, g_send),
        after,
    )


def hidden_kernel(g, w, slope, normed, box, box_n, total, own, own_n, send):
    for j in range(4):
        cols = slice(j * 512, (j + 1) * 512)
        grad = lax.dot_general(g[...], w[cols, :], ROWS_COLS, preferred_element_type=F32)
        low = rounded(grad * slope[j])
        box[j] = low
        total[:, cols] = jnp.sum(low, 0, keepdims=True)
    for c in (3, 0, 1, 2):
        arrange(
            lambda b: normed[c, :, b * 256 : (b + 1) * 256], own if c == 3 else own_n.at[c], send
        )
        out, at = (box, 4) if c == 3 else (box_n, 2 * c)
        pack(send, out.at[at], out.at[at + 1])


def grad_hidden_of(rows, w_fc2, slope, normed, after=()):
    return call(
        "grad_hidden",
        hidden_kernel,
        [VMEM] * 4,
        [
            shaped((6, SEQ, 512)),
            shaped((6, SEQ, 512)),
            shaped((1, D)),
            shaped((1024, SEQ), BF16),
            shaped((3, 1024, SEQ), BF16),
        ],
        (rows, w_fc2, slope, normed),
        after,
        [pltpu.VMEM((1024, SEQ), F32)],
    )


def in_ring_order(read):
    _, _, c, x = place()
    parts = []
    for r in (1, 2, 3, 0):
        at = pl.multiple_of(x_chunk(c, x, r) * QUARTER, QUARTER)
        parts.append(read(pl.ds(at, QUARTER)))
    return jnp.concatenate(parts, 0).astype(BF16)


def to_quarters(res, outs, part, cols):
    for k, out in enumerate(outs):
        out[part, :, cols] = res[k * QUARTER : (k + 1) * QUARTER]


def to_hbm(staged, n, outs, sems):
    copies = [
        pltpu.make_async_copy(
            staged.at[n % 2, pl.ds((k + 1) * QUARTER, QUARTER), :], out, sems.at[n * 3 + k]
        )
        for k, out in enumerate(outs)
    ]
    for copy in copies:
        copy.start()
    return copies


def settle(copies):
    for copy in copies:
        copy.wait()


def quarters(res, outs, cols):
    for k, out in enumerate(outs):
        out[:, cols] = res[k * QUARTER : (k + 1) * QUARTER]


def ffn_back_kernel(box, w, o1, o2, o3, o0, gh):
    blocks = [slice(j * 512, (j + 1) * 512) for j in range(4)]
    for j, cols in enumerate(blocks):
        gh[:, cols] = in_ring_order(lambda rows: box[j, rows, :])
    for cols in blocks:
        res = lax.dot_general(gh[...], w[cols, :], ROWS_COLS, preferred_element_type=F32)
        quarters(res, (o1, o2, o3, o0), cols)


def ffn_back(box_b, w_fc1, after=()):
    return call(
        "ffn_back",
        ffn_back_kernel,
        [VMEM] * 2,
        [shaped((QUARTER, D))] * 4,
        (box_b, w_fc1),
        after,
        [pltpu.VMEM((SEQ, D), BF16)],
    )


def branch_kernel(box_a, box_c, wo, w2, o1, o2, o3, o0, act):
    blocks = [slice(j * 512, (j + 1) * 512) for j in range(4)]
    for j, cols in enumerate(blocks):
        act[:, cols] = in_ring_order(lambda rows: box_a[j, rows, :])
    lhs = in_ring_order(lambda rows: box_c[0, rows, :])
    for cols in blocks:
        res = jnp.dot(lhs, wo[:, cols], preferred_element_type=F32)
        res = res + jnp.dot(act[...], w2[:, cols], preferred_element_type=F32)
        quarters(res, (o1, o2, o3, o0), cols)


def branches(box_a, box_c, w_out, w_fc2, after=()):
    return call(
        "branches",
        branch_kernel,
        [VMEM] * 4,
        [shaped((QUARTER, D))] * 4,
        (box_a, box_c, w_out, w_fc2),
        after,
        [pltpu.VMEM((SEQ, D), BF16)],
    )


def turn(v, cos, lead, tail, sign):
    return v * cos + sign * (pltpu.roll(v, HD - 16, 1) * lead + pltpu.roll(v, 16, 1) * tail)


def attn_kernel(
    length, normed, w, b, rows, wo, cos_ref, lead_ref, tail_ref,
    mid, total, o1, o2, o3, o0, staged, sems,
):
    scale = 1.0 / math.sqrt(HD)
    cos, lead, tail = cos_ref[...], lead_ref[...], tail_ref[...]
    at_q = lax.broadcasted_iota(jnp.int32, (SEQ, SEQ), 0)
    at_k = lax.broadcasted_iota(jnp.int32, (SEQ, SEQ), 1)
    allowed = (at_k <= at_q) & (at_k < length[0])
    for pair in range(2):
        wide = slice(pair * 2 * HD, (pair + 1) * 2 * HD)
        proj = [
            jnp.dot(normed[c], w[c, :, wide], preferred_element_type=F32) + b[c : c + 1, wide]
            for c in range(3)
        ]
        grad_ctx = lax.dot_general(rows[...], wo[wide, :], ROWS_COLS, preferred_element_type=F32)
        for n in range(2):
            cols = slice(n * HD, (n + 1) * HD)
            to = slice((pair * 2 + n) * HD, (pair * 2 + n + 1) * HD)
            q = turn(proj[0][:, cols], cos, lead, tail, 1.0).astype(BF16)
            k = turn(proj[1][:, cols], cos, lead, tail, 1.0).astype(BF16)
            v = proj[2][:, cols].astype(BF16)
            gc = grad_ctx[:, cols].astype(BF16)
            scores = lax.dot_general(q, k, ROWS_COLS, preferred_element_type=F32) * scale
            scores = jnp.where(allowed, scores, -1e30)
            weights = jnp.exp(scores - jnp.max(scores, -1, keepdims=True))
            probs = weights / jnp.sum(weights, -1, keepdims=True)
            low = probs.astype(BF16)
            mid[0, :, to] = rounded(jnp.dot(low, v, preferred_element_type=F32))
            gp = lax.dot_general(gc, v, ROWS_COLS, preferred_element_type=F32)
            gs = (probs * (gp - jnp.sum(probs * gp, -1, keepdims=True))).astype(BF16)
            gv = lax.dot_general(low, gc, ROWS_ROWS, preferred_element_type=F32)
            gq = jnp.dot(gs, k, preferred_element_type=F32) * scale
            gk = lax.dot_general(gs, q, ROWS_ROWS, preferred_element_type=F32) * scale
            grads = (turn(gq, cos, lead, tail, -1.0), turn(gk, cos, lead, tail, -1.0), gv)
            for c in range(3):
                g = rounded(grads[c])
                mid[c + 1, :, to] = g
                total[c : c + 1, to] = jnp.sum(g, 0, keepdims=True)
    sent = []
    for c in range(3):
        if c == 2:
            settle(sent[0])
        lhs = in_ring_order(lambda rows: mid[c + 1, rows, :])
        for j in range(4):
            cols = slice(j * 512, (j + 1) * 512)
            staged[c % 2, :, cols] = lax.dot_general(
                lhs, w[c, cols, :], ROWS_COLS, preferred_element_type=F32
            )
        o1[c] = staged[c % 2, :QUARTER]
        sent.append(to_hbm(staged, c, [out.at[c] for out in (o2, o3, o0)], sems))
    settle(sent[1] + sent[2])


def rotary():
    half = ROT // 2
    position = np.arange(SEQ, dtype=np.float32)
    freq_steps = np.arange(0, ROT, 2, dtype=np.float32) / np.float32(ROT)
    inverse = np.exp(freq_steps * np.float32(-math.log(10000.0)))
    angles = position[:, None] * inverse[None, :]
    cos, sin = np.cos(angles), np.sin(angles)
    wide = np.ones((SEQ, HD), np.float32)
    lead, tail = np.zeros((SEQ, HD), np.float32), np.zeros((SEQ, HD), np.float32)
    wide[:, :half], wide[:, half:ROT] = cos, cos
    lead[:, :half], tail[:, half:ROT] = -sin, sin
    return jnp.asarray(wide), jnp.asarray(lead), jnp.asarray(tail)


def attention(lengths, normed, w_t, b_qkv, rows, w_out, tables, after=()):
    return call(
        "attention",
        attn_kernel,
        [SMEM] + [VMEM] * 8,
        [shaped((4, SEQ, 512)), shaped((3, 512)), shaped((3, QUARTER, D))]
        + [pltpu.HBM((3, QUARTER, D), F32)] * 3,
        (lengths, normed, w_t, b_qkv, rows, w_out, *tables),
        after,
        [pltpu.VMEM((2, SEQ, D), F32), pltpu.SemaphoreType.DMA((9,))],
        out_specs=[VMEM] * 3 + [HBM] * 3,
    )


def wgrad_kernel(plan, n_in, *refs):
    up, down, hop, kept, *saved, staged, sems = refs[n_in:]
    made, last = None, None
    sent = []
    for j, (left, own, first, second, right, mate) in enumerate(plan(refs[:n_in])):
        cols = slice(j * 512, (j + 1) * 512)
        if left != last:
            made = own[...]
            if first is not None:
                made = jnp.concatenate([made, unpack(first, second)], 1)
            for out in saved:
                out[...] = made
        last = left
        both = jnp.concatenate([right[...].astype(BF16), mate[...].astype(BF16)], 0)
        res = jnp.dot(made, both, preferred_element_type=F32)
        up[:, cols] = res[:256]
        down[:, cols] = res[256:512]
        if j >= 2:
            for copy in sent[j - 2]:
                copy.wait()
        staged[j % 2] = res[512:]
        copies = [
            pltpu.make_async_copy(
                staged.at[j % 2, pl.ds(k * 256, 256), :],
                out.at[:, pl.ds(j * 512, 512)],
                sems.at[2 * j + k],
            )
            for k, out in enumerate((hop, kept))
        ]
        for copy in copies:
            copy.start()
        sent.append(copies)
    for copies in sent[2:]:
        for copy in copies:
            copy.wait()


def plan_a(refs):
    own, box, mate = refs
    return [(0, own, mate.at[4], mate.at[5], box.at[j], mate.at[j]) for j in range(4)]


def plan_b(refs):
    own, box, mate = refs
    return [(0, own, mate.at[4], mate.at[5], box.at[j], mate.at[j]) for j in range(4)]


def plan_c(refs):
    g_pair, own, box, mate, mate_n = refs
    out = [(0, g_pair, None, None, box.at[0], mate.at[0])]
    for c in range(3):
        parts = mate_n.at[2 * c], mate_n.at[2 * c + 1]
        out.append((c + 1, own.at[c], *parts, box.at[c + 1], mate.at[c + 1]))
    return out


def wgrad(name, plan, args, after=(), keep=False):
    return call(
        name,
        functools.partial(wgrad_kernel, plan, len(args)),
        [VMEM] * len(args),
        [shaped((256, D))] * 2 + [pltpu.HBM((256, D), F32)] * 2 + [shaped((1024, 512), BF16)] * keep,
        args,
        after,
        [pltpu.VMEM((2, 512, 512), F32), pltpu.SemaphoreType.DMA((8,))],
        out_specs=[VMEM] * 2 + [HBM] * 2 + [VMEM] * keep,
    )


def hold_kernel(a, out):
    out[...] = a[...]


def hold(name, a, after):
    return call(name, hold_kernel, [VMEM], shaped(a.shape), (a,), after)


def relay_kernel(*refs):
    *ins, up, down, out = refs
    for n in range(len(ins) // 4):
        hop, kept, up1, down1 = ins[4 * n : 4 * n + 4]
        cols = slice(n * D, (n + 1) * D)
        up[:, cols] = hop[:128] + up1[:128]
        down[:, cols] = hop[128:] + down1[:128]
        out[:128, cols] = kept[:128] + down1[128:]
        out[128:, cols] = kept[128:] + up1[128:]


def relay(name, pieces, after=()):
    args = [a for piece in pieces for a in piece]
    width = len(pieces) * D
    return call(
        name,
        relay_kernel,
        [VMEM] * len(args),
        [shaped((128, width)), shaped((128, width)), shaped((256, width))],
        args,
        after,
    )


def cross_kernel(kept, up2, down2, up, down, out):
    up[...] = kept[:64] + up2[:64]
    down[...] = kept[64:128] + up2[64:]
    out[...] = kept[128:] + down2[...]


def cross(name, kept, two, after=()):
    width = kept.shape[1]
    return call(
        name,
        cross_kernel,
        [VMEM] * 3,
        [shaped((64, width)), shaped((64, width)), shaped((128, width))],
        (kept, *two),
        after,
    )


def second_kernel(kept, got_up, got_down, up, down, out):
    up[...] = kept[:32] + got_up[:32]
    down[...] = kept[32:64] + got_down[:32]
    out[:32] = kept[64:96] + got_down[32:]
    out[32:] = kept[96:] + got_up[32:]


def second(name, kept, got_up, got_down, after=()):
    width = kept.shape[1]
    return call(
        name,
        second_kernel,
        [VMEM] * 3,
        [shaped((32, width)), shaped((32, width)), shaped((64, width))],
        (kept, got_up, got_down),
        after,
    )


def third_kernel(places, kept, last_up, last_down, *outs):
    for at, width, n, k in places:
        home = outs[n] if k is None else outs[n].at[k]
        cols = slice(at, at + width)
        home[:32] = kept[:32, cols] + last_up[:, cols]
        home[32:] = kept[32:, cols] + last_down[:, cols]


def third(name, places, out_shape, kept, last_up, last_down, after=()):
    return call(
        name,
        functools.partial(third_kernel, places),
        [VMEM] * 3,
        out_shape,
        (kept, last_up, last_down),
        after,
    )


def again_kernel(
    history, cotangent, mg, mi, mo, mb, hist, cot, hat, resid, wide, keep, left, stream, sems
):
    _, _, _, x = place()
    at = pl.ds(pl.multiple_of(x * QUARTER, QUARTER), QUARTER)
    copies = [
        pltpu.make_async_copy(history.at[:, at, :], hist, sems.at[0]),
        pltpu.make_async_copy(cotangent.at[at, :], cot, sems.at[1]),
    ]
    for copy in copies:
        copy.start()
    left[...] = split_in_three(mi[...] * mg[...])
    for copy in copies:
        copy.wait()
    inv, hid, slope, mw = mix_of(hist[HIST - 1], left[...], mo[...], mb[...])
    keep[:, 0:36] = hid
    keep[:, 128:164] = slope
    keep[:, 256:257] = inv
    for k in range(MIXH):
        wide[k] = jnp.broadcast_to(mw[:, k : k + 1], (QUARTER, 128))
    totals = blend(hist, block_diagonal(mw, spreading()), stream, QUARTER)
    for g in range(QUARTER // 16):
        rows = slice(g * 16, (g + 1) * 16)
        for c in range(STREAMS):
            mean, rstd = norm_parts(stream, totals, c, g)
            keep[rows, 257 + c : 258 + c] = rstd
            hat[c, rows] = (stream[c, rows] - mean) * rstd
    resid[...] = stream[STREAMS - 1]


def front_again(history, cotangent, mg, mi, mo, mb, after=()):
    return call(
        "front_again",
        again_kernel,
        [HBM, HBM] + [VMEM] * 4,
        [
            shaped((HIST, QUARTER, D), BF16),
            shaped((QUARTER, D), BF16),
            shaped((STREAMS, QUARTER, D)),
            shaped((QUARTER, D)),
            shaped((MIXH, QUARTER, 128)),
            shaped((QUARTER, 384)),
        ],
        (held(history), held(cotangent), mg, mi, mo, mb),
        after,
        [
            pltpu.VMEM((120, D), BF16),
            pltpu.VMEM((STREAMS, QUARTER, D), F32),
            pltpu.SemaphoreType.DMA((2,)),
        ],
    )


def back_kernel(
    hist, cot, hat_ref, keep, mine, others, mine_f, others_f, mg_ref, mi_ref, mo_ref, ng_ref,
    sum_hidden, sum_proj, sum_rows, tiles, stream, d_cur, sums, product,
):
    rows = QUARTER
    mg, mi, mo = mg_ref[...], mi_ref[...], mo_ref[...]
    hid, slope, inv = keep[:, 0:36], keep[:, 128:164], keep[:, 256:257]
    for c in range(STREAMS):
        g = mine[c] + others[c] if c < 3 else mine_f[...] + others_f[0]
        hat = hat_ref[c]
        rstd = keep[:, 257 + c : 258 + c]
        sums[36 + c : 37 + c, :] = jnp.sum(g * hat, 0, keepdims=True)
        sums[40 + c : 41 + c, :] = jnp.sum(g, 0, keepdims=True)
        gh = g * ng_ref[c : c + 1]
        ds = rstd * (
            gh - jnp.mean(gh, -1, keepdims=True) - hat * jnp.mean(gh * hat, -1, keepdims=True)
        )
        if c == 3:
            ds = ds + cot[...].astype(F32)
        stream[c] = ds
    for g in range(rows // 16):
        at_rows = slice(g * 16, (g + 1) * 16)
        for c in range(STREAMS):
            for j in range(HIST):
                acc = None
                for k in range(D // 256):
                    cols = slice(k * 256, (k + 1) * 256)
                    term = stream[c, at_rows, cols] * hist[j, at_rows, cols].astype(F32)
                    acc = term if acc is None else acc + term
                product[c * HIST + j, at_rows] = acc[:, :128] + acc[:, 128:]
    lane = lax.broadcasted_iota(jnp.int32, (rows, MIXH), 1)
    gm = jnp.zeros((rows, MIXH), F32)
    for k in range(MIXH):
        gm = jnp.where(lane == k, jnp.sum(product[k], -1, keepdims=True), gm)
    grad_mo = lax.dot_general(hid, gm, ROWS_ROWS, precision=HIGH, preferred_element_type=F32)
    d_pre = slope * lax.dot_general(
        gm, mo, ROWS_COLS, precision=HIGH, preferred_element_type=F32
    )
    low = (inv * d_pre).T
    pad = jnp.zeros((4, rows), F32)
    parts = []
    for _ in range(3):
        part = low.astype(BF16).astype(F32)
        parts += [part, pad]
        low = low - part
    turned_pre = jnp.concatenate(parts, 0).astype(BF16)
    cur_low = hist[HIST - 1]
    three = jnp.dot(turned_pre, cur_low, preferred_element_type=F32)
    outer = three[0:36] + three[40:76] + three[80:116]
    sums[:MIXH, :] = outer * mg
    sums[44:45, :] = jnp.sum(outer * mi, 0, keepdims=True)
    sums[45:56, :] = jnp.zeros((11, D), F32)
    _, _, _, x = place()
    sums[pl.ds(48 + x, 1), :] = sum_hidden[...]
    sums[52:55, pl.ds(pl.multiple_of(x * 512, 512), 512)] = sum_proj[...]
    sums[55:56, :] = jnp.where(x == 0, sum_rows[...], 0.0)
    for g in range(7):
        for t in range(16):
            tiles[g * 16 + t] = sums[g * 8 : (g + 1) * 8, t * 128 : (t + 1) * 128]
    tiles[112:128] = jnp.zeros((16, 8, 128), F32)
    for g in range(4):
        tiles[112 + g, :, :MIXH] = grad_mo[g * 8 : (g + 1) * 8]
    tiles[116, 0:4, :MIXH] = grad_mo[32:36]
    tiles[116, 4:5, :MIXH] = jnp.sum(gm, 0, keepdims=True)
    d_unit = jnp.dot(d_pre, mi * mg, precision=HIGH, preferred_element_type=F32)
    unit = cur_low.astype(F32) * inv
    d_cur[...] = inv * (d_unit - unit * jnp.mean(d_unit * unit, -1, keepdims=True))


def history_kernel(stream, d_cur, wide, grad_hist):
    span = 256
    for g in range(QUARTER // 16):
        at_rows = slice(g * 16, (g + 1) * 16)
        for k in range(D // span):
            cols = slice(k * span, (k + 1) * span)
            ds = [stream[c, at_rows, cols] for c in range(STREAMS)]
            for j in range(HIST):
                acc = d_cur[at_rows, cols] if j == HIST - 1 else None
                for c in range(STREAMS):
                    w = wide[c * HIST + j, at_rows]
                    term = ds[c] * jnp.concatenate([w] * (span // 128), axis=1)
                    acc = term if acc is None else acc + term
                grad_hist[j, at_rows, cols] = acc.astype(BF16)


def front_back(again, rings, mg, mi, mo, ng, early, after=()):
    hist, cot, hat, _, wide, keep = again
    tiles, stream, d_cur = call(
        "front_back",
        back_kernel,
        [VMEM] * 15,
        [shaped((128, 8, 128)), shaped((STREAMS, QUARTER, D)), shaped((QUARTER, D))],
        (hist, cot, hat, keep, *rings, mg, mi, mo, ng, *early),
        after,
        [pltpu.VMEM((56, D), F32), pltpu.VMEM((MIXH, QUARTER, 128), F32)],
    )
    grad_history = call(
        "grad_history",
        history_kernel,
        [VMEM] * 3,
        shaped((HIST, QUARTER, D), BF16),
        (stream, d_cur, wide),
    )
    return grad_history, tiles


def spread_kernel(each, out):
    out[...] = jnp.broadcast_to(jnp.sum(each[...], 0, keepdims=True), out.shape)


def open_kernel(total, b_qkv, b_fc1, b_out, gain, bias, mgain, m_in, m_out, m_bias, rows):
    for g in range(7):
        for t in range(16):
            rows[g * 8 : (g + 1) * 8, t * 128 : (t + 1) * 128] = total[g * 16 + t]
    m_in[...] = rows[:MIXH]
    gain[...] = rows[36:40]
    bias[...] = rows[40:44]
    mgain[...] = rows[44:45]
    for k in range(4):
        b_fc1[:, k * D : (k + 1) * D] = rows[48 + k : 49 + k]
    b_qkv[...] = rows[52:55]
    b_out[...] = rows[55:56]
    for g in range(4):
        m_out[g * 8 : (g + 1) * 8] = total[112 + g, :, :MIXH]
    m_out[32:36] = total[116, 0:4, :MIXH]
    m_bias[...] = total[116, 4:5, :MIXH]


def spread(tiles, after=()):
    each = lax.all_to_all(tiles, ALL, 0, 0, tiled=True)
    return call("spread", spread_kernel, [VMEM], shaped(tiles.shape), (each,), after)


def opened(mine, after=()):
    total = lax.all_to_all(mine, ALL, 0, 0, tiled=True)
    shapes = [(3, D), (1, 4 * D), (1, D), (STREAMS, D), (STREAMS, D), (1, D), (MIXH, D)]
    shapes += [(MIXH, MIXH), (1, MIXH)]
    return call(
        "open",
        open_kernel,
        [VMEM],
        [shaped(shape) for shape in shapes],
        (total,),
        after,
        [pltpu.VMEM((56, D), F32)],
    )


def out_kernel(length, own, part, resid, bias, out):
    _, _, _, x = place()
    at = lax.broadcasted_iota(jnp.int32, (QUARTER, 1), 0) + x * QUARTER
    valid = jnp.where(at < length[0], 1.0, 0.0)
    out[...] = rounded(resid[...] + valid * (own[...] + part[...] + bias[...]))


def out_rows(lengths, own, part, resid, bias, after=()):
    return call(
        "out_rows",
        out_kernel,
        [SMEM] + [VMEM] * 4,
        shaped((QUARTER, D)),
        (lengths, own, part, resid, bias),
        after,
    )


def gather_kernel(r1, r2, r3, r0, out):
    _, _, c, x = place()
    for r, ref in ((1, r1), (2, r2), (3, r3), (0, r0)):
        at = pl.multiple_of(x_chunk(c, x, r) * QUARTER, QUARTER)
        out[pl.ds(at, QUARTER), :] = ref[...].astype(BF16)


def gathered(parts, after=()):
    return call("gathered", gather_kernel, [VMEM] * 4, shaped((SEQ, D), BF16), parts, after)


def plus_kernel(a, b, out):
    out[...] = a[...] + b[...]


def plus_1_kernel(a, got, f, out):
    out[:3] = a[...] + got[...]
    out[3] = f[...]


def plus_2_kernel(a, got, f, b, out):
    out[:3] = a[...] + got[:3]
    out[3] = f[...] + got[3]
    out[4] = b[...]


def plus_3_kernel(f, b, got, out):
    out[0] = f[...] + got[3]
    out[1] = b[...] + got[4]


def plus_4_kernel(b, got, out):
    out[...] = b[...] + got[1]


def plus(name, kernel, args, lead, after=()):
    shape = (lead, QUARTER, D) if lead else (QUARTER, D)
    return call(name, kernel, [VMEM] * len(args), shaped(shape), args, after)


def local(
    history, lengths, cotangent, w_qkv, b_qkv, w_out, w_fc1, b_fc1, w_fc2, out_bias,
    norm_gain, norm_bias, mix_gain, mix_in, mix_out, mix_bias,
):
    mg, mi, mb = mix_gain[None], mix_in.T, mix_bias[None]
    w_t = w_qkv.transpose(1, 0, 2)

    normed, rows, g_own, g_send, sum_rows = front(
        lengths, history, cotangent, mg, mi, mix_out, mb, norm_gain, norm_bias
    )
    box_c, sum_proj, ring1, ring2, ring3, ring0 = attention(
        lengths, normed, w_t, b_qkv, rows, w_out, rotary()
    )
    mate_c = to_mate(box_c)
    others = to_x(ring1)
    box_a, slope = fc1(normed, w_fc1, b_fc1[None], g_send, (sum_proj,))
    mate_a = to_mate(box_a)
    box_b, box_n, sum_hidden, n3_own, n_own = grad_hidden_of(rows, w_fc2, slope, normed)
    mate_b = to_mate(box_b)
    mate_n = to_mate(box_n)
    plan = g_own, box_a, mate_a
    up, down, *a0, g_pair = wgrad("wgrad_a", plan_a, plan, (n_own, mate_c), True)
    a1 = to_yz(up, 1, 0), to_yz(down, -1, 0)
    f1, f2, f3, f0 = ffn_back(box_b, w_fc1, (up,))
    step = plus("plus_1", plus_1_kernel, (ring2, others, f1), 4)
    others = to_x(step)
    up, down, *b0 = wgrad("wgrad_b", plan_b, (n3_own, box_b, mate_b), (step, mate_n))
    b1 = to_yz(up, 1, 0), to_yz(down, -1, 0)
    br1, br2, br3, br0 = branches(box_a, box_c, w_out, w_fc2, (up,))
    plan = g_pair, n_own, box_c, mate_c, mate_n
    up, down, *c0 = wgrad("wgrad_c", plan_c, plan, (br1, *a1))
    c1 = to_yz(up, 1, 0), to_yz(down, -1, 0)
    again = front_again(history, cotangent, mg, mi, mix_out, mb, (up,))
    step = plus("plus_2", plus_2_kernel, (ring3, others, f2, br1), 5, (again[0],))
    others = to_x(step)
    up, down, kept_ab = relay("relay_ab", ((*a0, *a1), (*b0, *b1)), (step,))
    ab2 = to_yz(up, 1, 0), to_yz(down, -1, 0)
    step = plus("plus_3", plus_3_kernel, (f3, br2, others), 2, (up,))
    others_f = to_x(step)
    up, down, kept_c = relay("relay_c", ((*c0, *c1),), (step,))
    c2 = to_yz(up, 1, 0), to_yz(down, -1, 0)

    step = plus("plus_4", plus_4_kernel, (br3, others_f), 0, (up,))
    got = to_x(step)
    early = sum_hidden, sum_proj, sum_rows
    rings = ring0, others, f0, others_f
    grad_history, tiles = front_back(
        again, rings, mg, mi, mix_out, norm_gain, early, (step,)
    )
    up, down, kept_ab = cross("cross_ab", kept_ab, ab2, (tiles,))
    ab1 = to_yz(up, 1, 1), to_yz(down, -1, 1)
    mine = out_rows(lengths, br0, got, again[3], out_bias[None], (up,))
    got1 = to_x(mine)
    shared = spread(tiles, (mine,))
    up, down, kept_c = cross("cross_c", kept_c, c2, (shared,))
    c1 = to_yz(up, 1, 1), to_yz(down, -1, 1)
    got1 = hold("hold_1", got1, (up,))
    got2 = to_x(got1)
    small = opened(shared, (got1,))
    up, down, kept_ab = second("second_ab", kept_ab, *ab1, (small[0],))
    ab2 = to_yz(up, 1, 1), to_yz(down, -1, 1)
    got2 = hold("hold_2", got2, (up,))
    got3 = to_x(got2)
    up, down, kept_c = second("second_c", kept_c, *c1, (got2,))
    c2 = to_yz(up, 1, 1), to_yz(down, -1, 1)
    grad_fc2, grad_fc1 = third(
        "third_ab",
        ((0, D, 0, None), (D, D, 1, None)),
        [shaped((64, D))] * 2,
        kept_ab,
        *ab2,
        (up,),
    )
    places = [(0, 512, 0, None)] + [(512 * (c + 1), 512, 1, c) for c in range(3)]
    grad_out, grad_qkv = third(
        "third_c",
        places,
        [shaped((64, 512)), shaped((3, 64, 512))],
        kept_c,
        *c2,
        (grad_fc1,),
    )
    block_out = gathered((got1, got2, got3, mine))
    g_b_qkv, g_b_fc1, g_b_out, g_gain, g_bias, g_mgain, g_min, g_mout, g_mbias = small
    return (
        block_out,
        grad_history,
        grad_qkv.transpose(1, 0, 2),
        g_b_qkv,
        grad_out.T,
        grad_fc1,
        g_b_fc1[0],
        grad_fc2.T,
        g_b_out[0],
        g_gain,
        g_bias,
        g_mgain[0],
        g_min.T,
        g_mout,
        g_mbias[0],
    )


def solution(mesh):
    in_specs = (
        P(None, "dp", None),
        P("dp"),
        P("dp", None),
        P(None, None, "tensor"),
        P(None, "tensor"),
        P("tensor", None),
        P(None, "tensor"),
        P("tensor"),
        P("tensor", None),
        P(),
        P(),
        P(),
        P(),
        P(),
        P(),
        P(),
    )
    out_specs = (
        P("dp", None),
        P(None, ("dp", "tensor"), None),
        P("dp", None, "tensor"),
        P(),
        P("tensor", "dp"),
        P("dp", "tensor"),
        P(),
        P("tensor", "dp"),
        P(),
        P(),
        P(),
        P(),
        P(),
        P(),
        P(),
    )
    return jax.shard_map(local, mesh=mesh, in_specs=in_specs, out_specs=out_specs, check_vma=False)
```

```python
import functools
import math

import jax
import jax.numpy as jnp
import numpy as np
from jax import lax
from jax.experimental import pallas as pl
from jax.experimental.pallas import tpu as pltpu
from jax.sharding import PartitionSpec as P

D = 2048
HD = 128
ROT = 32
HIST = 9
STREAMS = 4
MIXH = 36
SEQ = 256
QUARTER = 64
F32 = jnp.float32
BF16 = jnp.bfloat16
HIGH = lax.Precision.HIGHEST
ROWS_COLS = (((1,), (1,)), ((), ()))
ROWS_ROWS = (((0,), (0,)), ((), ()))
ALL = ("dp", "tensor")


def place():
    dp = lax.axis_index("dp")
    return dp // 8, (dp // 2) % 4, dp % 2, lax.axis_index("tensor")


def dp_of(y, z, c):
    return ((y % 4) * 4 + z % 4) * 2 + c


def yz_pairs(step, phase):
    out = []
    for y in range(4):
        for z in range(4):
            for c in range(2):
                along_y = c == phase
                to = dp_of(y + step, z, c) if along_y else dp_of(y, z + step, c)
                out.append((dp_of(y, z, c), to))
    return out


def x_pairs(step):
    out = []
    for d in range(32):
        for x in range(4):
            out.append((d * 4 + x, d * 4 + (x + (step if d % 2 == 0 else 4 - step)) % 4))
    return out


def to_yz(a, step, phase):
    return lax.ppermute(a, "dp", yz_pairs(step, phase))


def to_x(a, step=1):
    return lax.ppermute(a, ALL, x_pairs(step))


def to_mate(a):
    return lax.ppermute(a, "dp", [(d, d ^ 1) for d in range(32)])


def x_chunk(c, x, r):
    return jnp.where(c == 0, x - r + 4, x + r) % 4


def gelu_parts(v):
    cdf = 0.5 * (1.0 + lax.erf(v * math.sqrt(0.5)))
    pdf = jnp.exp(-0.5 * v * v) * (1.0 / math.sqrt(2.0 * math.pi))
    return v * cdf, cdf + v * pdf


def rounded(v):
    return v.astype(BF16).astype(F32)


VMEM = pl.BlockSpec(memory_space=pltpu.VMEM)
SMEM = pl.BlockSpec(memory_space=pltpu.SMEM)
ANY = pl.BlockSpec(memory_space=pl.ANY)
HBM = pl.BlockSpec(memory_space=pltpu.HBM)


MIB = {"attention": 12, "grad_hidden": 8, "wgrad_a": 13, "wgrad_b": 13, "wgrad_c": 13, "fc1": 8, "ffn_back": 18, "branches": 18}


COST = {
    "plus_1": 1.0,
    "relay_ab": 8.0,
    "relay_c": 8.0,
    "cross": 3.0,
    "plus_4": 8.0,
    "out_rows": 3.0,
    "second": 3.0,
    "spread": 8.0,
    "gathered": 2.0,
    "third": 1.0,
    "open": 1.0,
}


def call(name, kernel, in_specs, out_shape, args, after=(), scratch=(), grid=(), out_specs=None, mib=None, aliases=None):
    n_in, n_after = len(in_specs), len(after)

    def body(*refs):
        kernel(*refs[:n_in], *refs[n_in + n_after :])

    if out_specs is None:
        out_specs = jax.tree.map(lambda _: VMEM, out_shape)
    return pl.pallas_call(
        body,
        name=name,
        grid=grid,
        in_specs=list(in_specs) + [ANY] * n_after,
        out_specs=out_specs,
        scratch_shapes=list(scratch),
        out_shape=out_shape,
        input_output_aliases=aliases or {},
        compiler_params=pltpu.CompilerParams(vmem_limit_bytes=(mib or MIB.get(name, 16)) * 1024 * 1024),
        cost_estimate=pl.CostEstimate(
            flops=int(COST.get(name, 0.01) * 1e9), bytes_accessed=1, transcendentals=0
        ),
    )(*args, *after)


def held(a):
    return pltpu.with_memory_space_constraint(a, pltpu.HBM)


def whole(shape):
    return pl.BlockSpec(shape, lambda *_: (0,) * len(shape))


def shaped(shape, dtype=F32):
    return jax.ShapeDtypeStruct(shape, dtype)


def split_in_three(w):
    pad = jnp.zeros((4, w.shape[1]), F32)
    parts = []
    for _ in range(3):
        low = w.astype(BF16).astype(F32)
        parts += [low, pad]
        w = w - low
    return jnp.concatenate(parts, 0).astype(BF16)


def mix_of(cur, left, mo, mb):
    wide = cur.astype(F32)
    inv = lax.rsqrt(jnp.mean(wide * wide, -1, keepdims=True) + 1e-06)
    pre = lax.dot_general(cur, left, ROWS_COLS, preferred_element_type=F32)
    pre = inv * (pre[:, 0:36] + pre[:, 40:76] + pre[:, 80:116])
    hid, slope = gelu_parts(pre)
    mw = jnp.dot(hid, mo, precision=HIGH, preferred_element_type=F32) + mb
    return inv, hid, slope, mw


SPREAD = 256


def spreading():
    row = lax.broadcasted_iota(jnp.int32, (MIXH, STREAMS * SPREAD), 0)
    col = lax.broadcasted_iota(jnp.int32, (MIXH, STREAMS * SPREAD), 1)
    at = col % SPREAD
    hit = (row == (col // SPREAD) * HIST + at // 16) & (at < HIST * 16)
    return hit.astype(F32).astype(BF16)


def block_diagonal(mw, spread):
    rows = mw.shape[0]
    row = lax.broadcasted_iota(jnp.int32, (rows, STREAMS * SPREAD), 0)
    col = lax.broadcasted_iota(jnp.int32, (rows, STREAMS * SPREAD), 1)
    same = row % 16 == col % 16
    high = mw.astype(BF16)
    low = (mw - high.astype(F32)).astype(BF16)
    out = []
    for part in (high, low):
        wide = jnp.dot(part, spread, preferred_element_type=F32)
        out.append(jnp.where(same, wide, 0.0).astype(BF16))
    return out


def blend(hist_ref, blocks, stream_ref, rows, start=0):
    totals = []
    for g in range(rows // 16):
        at = slice(g * 16, (g + 1) * 16)
        left = jnp.concatenate(
            [
                part[at, c * SPREAD : c * SPREAD + HIST * 16]
                for part in blocks
                for c in range(STREAMS)
            ],
            0,
        )
        total = None
        for k in range(D // 256):
            cols = slice(k * 256, (k + 1) * 256)
            right = jnp.concatenate(
                [hist_ref[j, pl.ds(start + g * 16, 16), cols] for j in range(HIST)], 0
            )
            res = jnp.dot(left, right, preferred_element_type=F32)
            res = res[: STREAMS * 16] + res[STREAMS * 16 :]
            for c in range(STREAMS):
                stream_ref[c, at, cols] = res[c * 16 : (c + 1) * 16]
            part = res[:, :128] + res[:, 128:]
            total = part if total is None else total + part
        totals.append(jnp.sum(total, -1, keepdims=True))
    return totals


def norm_parts(stream_ref, totals, c, g):
    at = slice(g * 16, (g + 1) * 16)
    mean = totals[g][c * 16 : (c + 1) * 16] * (1.0 / D)
    total = None
    for k in range(D // 256):
        cen = stream_ref[c, at, k * 256 : (k + 1) * 256] - mean
        sq = cen * cen
        part = sq[:, :128] + sq[:, 128:]
        total = part if total is None else total + part
    var = jnp.sum(total, -1, keepdims=True) * (1.0 / D)
    return mean, lax.rsqrt(var + 1e-05)


def front_kernel(
    length, history, cot, mg_in, mi_in, mo_in, mb_in, ng_in, nb_in,
    normed, rows_out, own, send, total,
    hist, mg, mi, mo, mb, ng, nb, left, spread, stream, sems, big_sems,
):
    rows = QUARTER
    small = [
        pltpu.make_async_copy(src, dst, sems.at[n])
        for n, (src, dst) in enumerate(
            ((mg_in, mg), (mi_in, mi), (mo_in, mo), (mb_in, mb), (ng_in, ng), (nb_in, nb))
        )
    ]
    big = [
        pltpu.make_async_copy(
            history.at[:, pl.ds(n * rows, rows), :],
            hist.at[:, pl.ds(n * rows, rows), :],
            big_sems.at[n],
        )
        for n in range(SEQ // rows)
    ]
    for copy in small + big:
        copy.start()
    rows_kernel(length, cot, rows_out, own, send, total)
    for copy in small:
        copy.wait()
    left[...] = split_in_three(mi[...] * mg[...])
    spread[...] = spreading()

    def chunk(n, carry):
        start = pl.multiple_of(n * rows, rows)
        pltpu.make_async_copy(
            history.at[:, pl.ds(start, rows), :],
            hist.at[:, pl.ds(start, rows), :],
            big_sems.at[n],
        ).wait()
        _, _, _, mw = mix_of(hist[HIST - 1, pl.ds(start, rows)], left[...], mo[...], mb[...])
        totals = blend(hist, block_diagonal(mw, spread[...]), stream, rows, start)
        for g in range(rows // 16):
            at = slice(g * 16, (g + 1) * 16)
            for c in range(STREAMS):
                mean, rstd = norm_parts(stream, totals, c, g)
                for k in range(D // 512):
                    cols = slice(k * 512, (k + 1) * 512)
                    cen = stream[c, at, cols] - mean
                    normed[c, pl.ds(start + g * 16, 16), cols] = (
                        cen * rstd * ng[c : c + 1, cols] + nb[c : c + 1, cols]
                    ).astype(BF16)
        return carry

    lax.fori_loop(0, SEQ // rows, chunk, 0)


def front(lengths, history, cotangent, mg, mi, mo, mb, ng, nb):
    return call(
        "front",
        front_kernel,
        [SMEM, HBM, VMEM] + [HBM] * 6,
        [
            shaped((STREAMS, SEQ, D), BF16),
            shaped((SEQ, D), BF16),
            shaped((1024, SEQ), BF16),
            shaped((1024, SEQ)),
            shaped((1, D)),
        ],
        (lengths, held(history), cotangent, *map(held, (mg, mi, mo, mb, ng, nb))),
        (),
        [
            pltpu.VMEM((HIST, SEQ, D), BF16),
            pltpu.VMEM((1, D), F32),
            pltpu.VMEM((MIXH, D), F32),
            pltpu.VMEM((MIXH, MIXH), F32),
            pltpu.VMEM((1, MIXH), F32),
            pltpu.VMEM((STREAMS, D), F32),
            pltpu.VMEM((STREAMS, D), F32),
            pltpu.VMEM((120, D), BF16),
            pltpu.VMEM((MIXH, STREAMS * SPREAD), BF16),
            pltpu.VMEM((STREAMS, QUARTER, D), F32),
            pltpu.SemaphoreType.DMA((6,)),
            pltpu.SemaphoreType.DMA((4,)),
        ],
        mib=24,
    )


def slot(r, h):
    first = jnp.where(r == 0, 6, jnp.where(r == 1, 4, jnp.where(r == 2, 0, 3)))
    second = jnp.where(r == 0, 7, jnp.where(r == 1, 1, jnp.where(r == 2, 2, 5)))
    return jnp.where(h == 0, first, second)


def pick(c):
    row = lax.broadcasted_iota(jnp.int32, (128, 256), 0)
    col = lax.broadcasted_iota(jnp.int32, (128, 256), 1)
    return (col == (row // 64) * 128 + c * 64 + row % 64).astype(F32).astype(BF16)


def arrange(read, own, send):
    y0, z0, c0, _ = place()
    for c, out in ((c0, own), (1 - c0, send)):
        chosen = pick(c)
        for b in range(8):
            flipped = lax.dot_general(chosen, read(b), ROWS_COLS, preferred_element_type=F32)
            for part in range(4):
                y, z, h = b // 2, (b % 2) * 2 + part // 2, part % 2
                dy, dz = (y - y0 + 4) % 4, (z - z0 + 4) % 4
                r1, r2 = jnp.where(c == 0, dy, dz), jnp.where(c == 0, dz, dy)
                inner = slot(r2, h)
                at = pl.multiple_of((slot(r1, inner // 4) * 4 + inner % 4) * 32, 32)
                out[pl.ds(at, 32), :] = flipped[part * 32 : (part + 1) * 32].astype(out.dtype)


def rows_kernel(length, cot, rows_out, own, send, total):
    at = lax.broadcasted_iota(jnp.int32, (SEQ, 1), 0)
    for k in range(8):
        cols = slice(k * 256, (k + 1) * 256)
        g = jnp.where(at < length[0], cot[:, cols].astype(F32), 0.0)
        rows_out[:, cols] = g.astype(BF16)
        total[:, cols] = jnp.sum(g, 0, keepdims=True)
    arrange(lambda b: rows_out[:, b * 256 : (b + 1) * 256], own, send)


def pack(rows, first, second):
    for k in range(4):
        out = first if k < 2 else second
        out[:, (k % 2) * 256 : (k % 2 + 1) * 256] = rows[k * 256 : (k + 1) * 256]


def unpack(first, second):
    pieces = [
        out[:, k * 256 : (k + 1) * 256].astype(BF16) for out in (first, second) for k in range(2)
    ]
    return jnp.concatenate(pieces, 0)


def fc1_kernel(x, w, b, g_send, box, slope):
    for j in range(4):
        cols = slice(j * 512, (j + 1) * 512)
        pre = jnp.dot(x[3], w[:, cols], preferred_element_type=F32) + b[:, cols]
        value, grad = gelu_parts(pre)
        box[j] = rounded(value)
        slope[j] = grad
    pack(g_send, box.at[4], box.at[5])


def fc1(normed, w_fc1, b_fc1, g_send, after=()):
    return call(
        "fc1",
        fc1_kernel,
        [VMEM] * 4,
        [shaped((6, SEQ, 512)), shaped((4, SEQ, 512))],
        (normed, w_fc1, b_fc1, g_send),
        after,
    )


def hidden_kernel(g, w, slope, normed, box, box_n, total, own, own_n, send):
    for j in range(4):
        cols = slice(j * 512, (j + 1) * 512)
        grad = lax.dot_general(g[...], w[cols, :], ROWS_COLS, preferred_element_type=F32)
        low = rounded(grad * slope[j])
        box[j] = low
        total[:, cols] = jnp.sum(low, 0, keepdims=True)
    for c in (3, 0, 1, 2):
        arrange(
            lambda b: normed[c, :, b * 256 : (b + 1) * 256], own if c == 3 else own_n.at[c], send
        )
        out, at = (box, 4) if c == 3 else (box_n, 2 * c)
        pack(send, out.at[at], out.at[at + 1])


def grad_hidden_of(rows, w_fc2, slope, normed, after=()):
    return call(
        "grad_hidden",
        hidden_kernel,
        [VMEM] * 4,
        [
            shaped((6, SEQ, 512)),
            shaped((6, SEQ, 512)),
            shaped((1, D)),
            shaped((1024, SEQ), BF16),
            shaped((3, 1024, SEQ), BF16),
        ],
        (rows, w_fc2, slope, normed),
        after,
        [pltpu.VMEM((1024, SEQ), F32)],
    )


def in_ring_order(read):
    _, _, c, x = place()
    parts = []
    for r in (1, 2, 3, 0):
        at = pl.multiple_of(x_chunk(c, x, r) * QUARTER, QUARTER)
        parts.append(read(pl.ds(at, QUARTER)))
    return jnp.concatenate(parts, 0).astype(BF16)


def to_quarters(res, outs, part, cols):
    for k, out in enumerate(outs):
        out[part, :, cols] = res[k * QUARTER : (k + 1) * QUARTER]


def to_hbm(staged, n, outs, sems):
    copies = [
        pltpu.make_async_copy(
            staged.at[n % 2, pl.ds((k + 1) * QUARTER, QUARTER), :], out, sems.at[n * 3 + k]
        )
        for k, out in enumerate(outs)
    ]
    for copy in copies:
        copy.start()
    return copies


def settle(copies):
    for copy in copies:
        copy.wait()


def quarters(res, outs, cols):
    for k, out in enumerate(outs):
        out[:, cols] = res[k * QUARTER : (k + 1) * QUARTER]


def streamed(w, slots, sems):
    copies = [
        pltpu.make_async_copy(w.at[pl.ds(j * 512, 512), :], slots.at[j], sems.at[j])
        for j in range(4)
    ]
    for copy in copies:
        copy.start()
    return copies


def ffn_back_kernel(box, w, o1, o2, o3, o0, gh, slots, sems):
    copies = streamed(w, slots, sems)
    blocks = [slice(j * 512, (j + 1) * 512) for j in range(4)]
    for j, cols in enumerate(blocks):
        gh[:, cols] = in_ring_order(lambda rows: box[j, rows, :])
    for j, cols in enumerate(blocks):
        copies[j].wait()
        res = lax.dot_general(gh[...], slots[j], ROWS_COLS, preferred_element_type=F32)
        quarters(res, (o1, o2, o3, o0), cols)


STREAM = [
    pltpu.VMEM((SEQ, D), BF16),
    pltpu.VMEM((4, 512, D), BF16),
    pltpu.SemaphoreType.DMA((4,)),
]


def ffn_back(box_b, w_fc1, after=()):
    return call(
        "ffn_back",
        ffn_back_kernel,
        [VMEM, HBM],
        [shaped((QUARTER, D))] * 4,
        (box_b, held(w_fc1)),
        after,
        STREAM,
    )


def branch_kernel(box_a, box_c, wo, w2, o1, o2, o3, o0, act, slots, sems):
    copies = streamed(w2, slots, sems)
    blocks = [slice(j * 512, (j + 1) * 512) for j in range(4)]
    for j, cols in enumerate(blocks):
        act[:, cols] = in_ring_order(lambda rows: box_a[j, rows, :])
    lhs = in_ring_order(lambda rows: box_c[0, rows, :])
    for copy in copies:
        copy.wait()
    for cols in blocks:
        res = jnp.dot(lhs, wo[:, cols], preferred_element_type=F32)
        for j, k in enumerate(blocks):
            res = res + jnp.dot(act[:, k], slots[j, :, cols], preferred_element_type=F32)
        quarters(res, (o1, o2, o3, o0), cols)


def branches(box_a, box_c, w_out, w_fc2, after=()):
    return call(
        "branches",
        branch_kernel,
        [VMEM] * 3 + [HBM],
        [shaped((QUARTER, D))] * 4,
        (box_a, box_c, w_out, held(w_fc2)),
        after,
        STREAM,
    )


def turn(v, cos, lead, tail, sign):
    return v * cos + sign * (pltpu.roll(v, HD - 16, 1) * lead + pltpu.roll(v, 16, 1) * tail)


def attn_kernel(
    length, normed, w, b, rows, wo, cos_ref, lead_ref, tail_ref,
    mid, total, o1, o2, o3, o0, staged, sems,
):
    scale = 1.0 / math.sqrt(HD)
    cos, lead, tail = cos_ref[...], lead_ref[...], tail_ref[...]
    at_q = lax.broadcasted_iota(jnp.int32, (SEQ, SEQ), 0)
    at_k = lax.broadcasted_iota(jnp.int32, (SEQ, SEQ), 1)
    allowed = (at_k <= at_q) & (at_k < length[0])
    for pair in range(2):
        wide = slice(pair * 2 * HD, (pair + 1) * 2 * HD)
        proj = [
            jnp.dot(normed[c], w[c, :, wide], preferred_element_type=F32) + b[c : c + 1, wide]
            for c in range(3)
        ]
        grad_ctx = lax.dot_general(rows[...], wo[wide, :], ROWS_COLS, preferred_element_type=F32)
        for n in range(2):
            cols = slice(n * HD, (n + 1) * HD)
            to = slice((pair * 2 + n) * HD, (pair * 2 + n + 1) * HD)
            q = turn(proj[0][:, cols], cos, lead, tail, 1.0).astype(BF16)
            k = turn(proj[1][:, cols], cos, lead, tail, 1.0).astype(BF16)
            v = proj[2][:, cols].astype(BF16)
            gc = grad_ctx[:, cols].astype(BF16)
            scores = lax.dot_general(q, k, ROWS_COLS, preferred_element_type=F32) * scale
            scores = jnp.where(allowed, scores, -1e30)
            weights = jnp.exp(scores - jnp.max(scores, -1, keepdims=True))
            probs = weights / jnp.sum(weights, -1, keepdims=True)
            low = probs.astype(BF16)
            mid[0, :, to] = rounded(jnp.dot(low, v, preferred_element_type=F32))
            gp = lax.dot_general(gc, v, ROWS_COLS, preferred_element_type=F32)
            gs = (probs * (gp - jnp.sum(probs * gp, -1, keepdims=True))).astype(BF16)
            gv = lax.dot_general(low, gc, ROWS_ROWS, preferred_element_type=F32)
            gq = jnp.dot(gs, k, preferred_element_type=F32) * scale
            gk = lax.dot_general(gs, q, ROWS_ROWS, preferred_element_type=F32) * scale
            grads = (turn(gq, cos, lead, tail, -1.0), turn(gk, cos, lead, tail, -1.0), gv)
            for c in range(3):
                g = rounded(grads[c])
                mid[c + 1, :, to] = g
                total[c : c + 1, to] = jnp.sum(g, 0, keepdims=True)
    sent = []
    for c in range(3):
        if c == 2:
            settle(sent[0])
        lhs = in_ring_order(lambda rows: mid[c + 1, rows, :])
        for j in range(4):
            cols = slice(j * 512, (j + 1) * 512)
            staged[c % 2, :, cols] = lax.dot_general(
                lhs, w[c, cols, :], ROWS_COLS, preferred_element_type=F32
            )
        o1[c] = staged[c % 2, :QUARTER]
        sent.append(to_hbm(staged, c, [out.at[c] for out in (o2, o3, o0)], sems))
    settle(sent[1] + sent[2])


def rotary():
    half = ROT // 2
    position = np.arange(SEQ, dtype=np.float32)
    freq_steps = np.arange(0, ROT, 2, dtype=np.float32) / np.float32(ROT)
    inverse = np.exp(freq_steps * np.float32(-math.log(10000.0)))
    angles = position[:, None] * inverse[None, :]
    cos, sin = np.cos(angles), np.sin(angles)
    wide = np.ones((SEQ, HD), np.float32)
    lead, tail = np.zeros((SEQ, HD), np.float32), np.zeros((SEQ, HD), np.float32)
    wide[:, :half], wide[:, half:ROT] = cos, cos
    lead[:, :half], tail[:, half:ROT] = -sin, sin
    return jnp.asarray(wide), jnp.asarray(lead), jnp.asarray(tail)


def attention(lengths, normed, w_t, b_qkv, rows, w_out, tables, after=()):
    return call(
        "attention",
        attn_kernel,
        [SMEM] + [VMEM] * 8,
        [shaped((4, SEQ, 512)), shaped((3, 512)), shaped((3, QUARTER, D))]
        + [pltpu.HBM((3, QUARTER, D), F32)] * 3,
        (lengths, normed, w_t, b_qkv, rows, w_out, *tables),
        after,
        [pltpu.VMEM((2, SEQ, D), F32), pltpu.SemaphoreType.DMA((9,))],
        out_specs=[VMEM] * 3 + [HBM] * 3,
    )


def wgrad_kernel(plan, n_in, *refs):
    up, down, hop, kept, *saved, staged, sems = refs[n_in:]
    made, last = None, None
    sent = []
    for j, (left, own, first, second, right, mate) in enumerate(plan(refs[:n_in])):
        cols = slice(j * 512, (j + 1) * 512)
        if left != last:
            made = own[...]
            if first is not None:
                made = jnp.concatenate([made, unpack(first, second)], 1)
            for out in saved:
                out[...] = made
        last = left
        both = jnp.concatenate([right[...].astype(BF16), mate[...].astype(BF16)], 0)
        res = jnp.dot(made, both, preferred_element_type=F32)
        up[:, cols] = res[:256]
        down[:, cols] = res[256:512]
        if j >= 2:
            for copy in sent[j - 2]:
                copy.wait()
        staged[j % 2] = res[512:]
        copies = [
            pltpu.make_async_copy(
                staged.at[j % 2, pl.ds(k * 256, 256), :],
                out.at[:, pl.ds(j * 512, 512)],
                sems.at[2 * j + k],
            )
            for k, out in enumerate((hop, kept))
        ]
        for copy in copies:
            copy.start()
        sent.append(copies)
    for copies in sent[2:]:
        for copy in copies:
            copy.wait()


def plan_a(refs):
    own, box, mate = refs
    return [(0, own, mate.at[4], mate.at[5], box.at[j], mate.at[j]) for j in range(4)]


def plan_b(refs):
    own, box, mate = refs
    return [(0, own, mate.at[4], mate.at[5], box.at[j], mate.at[j]) for j in range(4)]


def plan_c(refs):
    g_pair, own, box, mate, mate_n = refs
    out = [(0, g_pair, None, None, box.at[0], mate.at[0])]
    for c in range(3):
        parts = mate_n.at[2 * c], mate_n.at[2 * c + 1]
        out.append((c + 1, own.at[c], *parts, box.at[c + 1], mate.at[c + 1]))
    return out


def wgrad(name, plan, args, after=(), keep=False):
    return call(
        name,
        functools.partial(wgrad_kernel, plan, len(args)),
        [VMEM] * len(args),
        [shaped((256, D))] * 2 + [pltpu.HBM((256, D), F32)] * 2 + [shaped((1024, 512), BF16)] * keep,
        args,
        after,
        [pltpu.VMEM((2, 512, 512), F32), pltpu.SemaphoreType.DMA((8,))],
        out_specs=[VMEM] * 2 + [HBM] * 2 + [VMEM] * keep,
    )


def relay_kernel(*refs):
    *ins, up, down, out = refs
    for n in range(len(ins) // 4):
        hop, kept, up1, down1 = ins[4 * n : 4 * n + 4]
        cols = slice(n * D, (n + 1) * D)
        up[:, cols] = hop[:128] + up1[:128]
        down[:, cols] = hop[128:] + down1[:128]
        out[:128, cols] = kept[:128] + down1[128:]
        out[128:, cols] = kept[128:] + up1[128:]


def relay(name, pieces, after=()):
    args = [a for piece in pieces for a in piece]
    width = len(pieces) * D
    return call(
        name,
        relay_kernel,
        [VMEM] * len(args),
        [shaped((128, width)), shaped((128, width)), shaped((256, width))],
        args,
        after,
    )


def cross_kernel(*refs):
    *ins, up, down, out = refs
    at = 0
    for n in range(len(ins) // 3):
        kept, up2, down2 = ins[3 * n : 3 * n + 3]
        cols = slice(at, at + kept.shape[1])
        at += kept.shape[1]
        up[:, cols] = kept[:64] + up2[:64]
        down[:, cols] = kept[64:128] + up2[64:]
        out[:, cols] = kept[128:] + down2[...]


def cross(name, pieces, after=()):
    args = [a for piece in pieces for a in piece]
    width = sum(piece[0].shape[1] for piece in pieces)
    return call(
        name,
        cross_kernel,
        [VMEM] * len(args),
        [shaped((64, width)), shaped((64, width)), shaped((128, width))],
        args,
        after,
    )


def second_kernel(kept, got_up, got_down, up, down, out):
    up[...] = kept[:32] + got_up[:32]
    down[...] = kept[32:64] + got_down[:32]
    out[:32] = kept[64:96] + got_down[32:]
    out[32:] = kept[96:] + got_up[32:]


def second(name, kept, got_up, got_down, after=()):
    width = kept.shape[1]
    return call(
        name,
        second_kernel,
        [VMEM] * 3,
        [shaped((32, width)), shaped((32, width)), shaped((64, width))],
        (kept, got_up, got_down),
        after,
    )


def third_kernel(places, kept, last_up, last_down, *outs):
    for at, width, n, k in places:
        home = outs[n] if k is None else outs[n].at[k]
        cols = slice(at, at + width)
        home[:32] = kept[:32, cols] + last_up[:, cols]
        home[32:] = kept[32:, cols] + last_down[:, cols]


def third(name, places, out_shape, kept, last_up, last_down, after=()):
    return call(
        name,
        functools.partial(third_kernel, places),
        [VMEM] * 3,
        out_shape,
        (kept, last_up, last_down),
        after,
    )


def again_kernel(
    history, cotangent, mg, mi, mo, mb, hist, cot, hat, resid, wide, keep, left, stream, sems
):
    _, _, _, x = place()
    at = pl.ds(pl.multiple_of(x * QUARTER, QUARTER), QUARTER)
    copies = [
        pltpu.make_async_copy(history.at[:, at, :], hist, sems.at[0]),
        pltpu.make_async_copy(cotangent.at[at, :], cot, sems.at[1]),
    ]
    for copy in copies:
        copy.start()
    left[...] = split_in_three(mi[...] * mg[...])
    for copy in copies:
        copy.wait()
    inv, hid, slope, mw = mix_of(hist[HIST - 1], left[...], mo[...], mb[...])
    keep[:, 0:36] = hid
    keep[:, 128:164] = slope
    keep[:, 256:257] = inv
    for k in range(MIXH):
        wide[k] = jnp.broadcast_to(mw[:, k : k + 1], (QUARTER, 128))
    totals = blend(hist, block_diagonal(mw, spreading()), stream, QUARTER)
    for g in range(QUARTER // 16):
        rows = slice(g * 16, (g + 1) * 16)
        for c in range(STREAMS):
            mean, rstd = norm_parts(stream, totals, c, g)
            keep[rows, 257 + c : 258 + c] = rstd
            hat[c, rows] = (stream[c, rows] - mean) * rstd
    resid[...] = stream[STREAMS - 1]


def front_again(history, cotangent, mg, mi, mo, mb, after=()):
    return call(
        "front_again",
        again_kernel,
        [HBM, HBM] + [VMEM] * 4,
        [
            shaped((HIST, QUARTER, D), BF16),
            shaped((QUARTER, D), BF16),
            shaped((STREAMS, QUARTER, D)),
            shaped((QUARTER, D)),
            shaped((MIXH, QUARTER, 128)),
            shaped((QUARTER, 384)),
        ],
        (held(history), held(cotangent), mg, mi, mo, mb),
        after,
        [
            pltpu.VMEM((120, D), BF16),
            pltpu.VMEM((STREAMS, QUARTER, D), F32),
            pltpu.SemaphoreType.DMA((2,)),
        ],
    )


def back_kernel(
    hist, cot, hat_ref, keep, mine, others, mine_f, others_f, mg_ref, mi_ref, mo_ref, ng_ref,
    sum_hidden, sum_proj, sum_rows, tiles, stream, d_cur, sums, product,
):
    rows = QUARTER
    mg, mi, mo = mg_ref[...], mi_ref[...], mo_ref[...]
    hid, slope, inv = keep[:, 0:36], keep[:, 128:164], keep[:, 256:257]
    for c in range(STREAMS):
        g = mine[c] + others[c] if c < 3 else mine_f[...] + others_f[0]
        hat = hat_ref[c]
        rstd = keep[:, 257 + c : 258 + c]
        sums[36 + c : 37 + c, :] = jnp.sum(g * hat, 0, keepdims=True)
        sums[40 + c : 41 + c, :] = jnp.sum(g, 0, keepdims=True)
        gh = g * ng_ref[c : c + 1]
        ds = rstd * (
            gh - jnp.mean(gh, -1, keepdims=True) - hat * jnp.mean(gh * hat, -1, keepdims=True)
        )
        if c == 3:
            ds = ds + cot[...].astype(F32)
        stream[c] = ds
    for g in range(rows // 16):
        at_rows = slice(g * 16, (g + 1) * 16)
        for c in range(STREAMS):
            for j in range(HIST):
                acc = None
                for k in range(D // 256):
                    cols = slice(k * 256, (k + 1) * 256)
                    term = stream[c, at_rows, cols] * hist[j, at_rows, cols].astype(F32)
                    acc = term if acc is None else acc + term
                product[c * HIST + j, at_rows] = acc[:, :128] + acc[:, 128:]
    lane = lax.broadcasted_iota(jnp.int32, (rows, MIXH), 1)
    gm = jnp.zeros((rows, MIXH), F32)
    for k in range(MIXH):
        gm = jnp.where(lane == k, jnp.sum(product[k], -1, keepdims=True), gm)
    grad_mo = lax.dot_general(hid, gm, ROWS_ROWS, precision=HIGH, preferred_element_type=F32)
    d_pre = slope * lax.dot_general(
        gm, mo, ROWS_COLS, precision=HIGH, preferred_element_type=F32
    )
    low = (inv * d_pre).T
    pad = jnp.zeros((4, rows), F32)
    parts = []
    for _ in range(3):
        part = low.astype(BF16).astype(F32)
        parts += [part, pad]
        low = low - part
    turned_pre = jnp.concatenate(parts, 0).astype(BF16)
    cur_low = hist[HIST - 1]
    three = jnp.dot(turned_pre, cur_low, preferred_element_type=F32)
    outer = three[0:36] + three[40:76] + three[80:116]
    sums[:MIXH, :] = outer * mg
    sums[44:45, :] = jnp.sum(outer * mi, 0, keepdims=True)
    sums[45:56, :] = jnp.zeros((11, D), F32)
    _, _, _, x = place()
    sums[pl.ds(48 + x, 1), :] = sum_hidden[...]
    sums[52:55, pl.ds(pl.multiple_of(x * 512, 512), 512)] = sum_proj[...]
    sums[55:56, :] = jnp.where(x == 0, sum_rows[...], 0.0)
    for g in range(7):
        for t in range(16):
            tiles[g * 16 + t] = sums[g * 8 : (g + 1) * 8, t * 128 : (t + 1) * 128]
    tiles[112:128] = jnp.zeros((16, 8, 128), F32)
    for g in range(4):
        tiles[112 + g, :, :MIXH] = grad_mo[g * 8 : (g + 1) * 8]
    tiles[116, 0:4, :MIXH] = grad_mo[32:36]
    tiles[116, 4:5, :MIXH] = jnp.sum(gm, 0, keepdims=True)
    d_unit = jnp.dot(d_pre, mi * mg, precision=HIGH, preferred_element_type=F32)
    unit = cur_low.astype(F32) * inv
    d_cur[...] = inv * (d_unit - unit * jnp.mean(d_unit * unit, -1, keepdims=True))


def history_kernel(stream, d_cur, wide, grad_hist):
    span = 256
    for g in range(QUARTER // 16):
        at_rows = slice(g * 16, (g + 1) * 16)
        for k in range(D // span):
            cols = slice(k * span, (k + 1) * span)
            ds = [stream[c, at_rows, cols] for c in range(STREAMS)]
            for j in range(HIST):
                acc = d_cur[at_rows, cols] if j == HIST - 1 else None
                for c in range(STREAMS):
                    w = wide[c * HIST + j, at_rows]
                    term = ds[c] * jnp.concatenate([w] * (span // 128), axis=1)
                    acc = term if acc is None else acc + term
                grad_hist[j, at_rows, cols] = acc.astype(BF16)


def front_back(again, rings, mg, mi, mo, ng, early, after=()):
    hist, cot, hat, _, _, keep = again
    return call(
        "front_back",
        back_kernel,
        [VMEM] * 15,
        [shaped((128, 8, 128)), shaped((STREAMS, QUARTER, D)), shaped((QUARTER, D))],
        (hist, cot, hat, keep, *rings, mg, mi, mo, ng, *early),
        after,
        [pltpu.VMEM((56, D), F32), pltpu.VMEM((MIXH, QUARTER, 128), F32)],
    )


def grad_history_of(stream, d_cur, wide, after=()):
    return call(
        "grad_history",
        history_kernel,
        [VMEM] * 3,
        shaped((HIST, QUARTER, D), BF16),
        (stream, d_cur, wide),
        after,
    )


def spread_kernel(each, out):
    out[...] = jnp.broadcast_to(jnp.sum(each[...], 0, keepdims=True), out.shape)


def open_kernel(total, b_qkv, b_fc1, b_out, gain, bias, mgain, m_in, m_out, m_bias, rows):
    for g in range(7):
        for t in range(16):
            rows[g * 8 : (g + 1) * 8, t * 128 : (t + 1) * 128] = total[g * 16 + t]
    m_in[...] = rows[:MIXH]
    gain[...] = rows[36:40]
    bias[...] = rows[40:44]
    mgain[...] = rows[44:45]
    for k in range(4):
        b_fc1[:, k * D : (k + 1) * D] = rows[48 + k : 49 + k]
    b_qkv[...] = rows[52:55]
    b_out[...] = rows[55:56]
    for g in range(4):
        m_out[g * 8 : (g + 1) * 8] = total[112 + g, :, :MIXH]
    m_out[32:36] = total[116, 0:4, :MIXH]
    m_bias[...] = total[116, 4:5, :MIXH]


def spread(tiles, after=()):
    each = lax.all_to_all(tiles, ALL, 0, 0, tiled=True)
    return call("spread", spread_kernel, [VMEM], shaped(tiles.shape), (each,), after)


def opened(mine, after=()):
    total = lax.all_to_all(mine, ALL, 0, 0, tiled=True)
    shapes = [(3, D), (1, 4 * D), (1, D), (STREAMS, D), (STREAMS, D), (1, D), (MIXH, D)]
    shapes += [(MIXH, MIXH), (1, MIXH)]
    return call(
        "open",
        open_kernel,
        [VMEM],
        [shaped(shape) for shape in shapes],
        (total,),
        after,
        [pltpu.VMEM((56, D), F32)],
    )


def out_kernel(length, own, part, resid, bias, out):
    _, _, _, x = place()
    at = lax.broadcasted_iota(jnp.int32, (QUARTER, 1), 0) + x * QUARTER
    valid = jnp.where(at < length[0], 1.0, 0.0)
    out[...] = rounded(resid[...] + valid * (own[...] + part[...] + bias[...]))


def out_rows(lengths, own, part, resid, bias, after=()):
    return call(
        "out_rows",
        out_kernel,
        [SMEM] + [VMEM] * 4,
        shaped((QUARTER, D)),
        (lengths, own, part, resid, bias),
        after,
    )


def gather_kernel(r1, r2, r3, r0, out):
    _, _, c, x = place()
    for r, ref in ((1, r1), (2, r2), (3, r3), (0, r0)):
        at = pl.multiple_of(x_chunk(c, x, r) * QUARTER, QUARTER)
        out[pl.ds(at, QUARTER), :] = ref[...].astype(BF16)


def gathered(parts, after=()):
    return call("gathered", gather_kernel, [VMEM] * 4, shaped((SEQ, D), BF16), parts, after)


def plus_kernel(a, b, out):
    out[...] = a[...] + b[...]


def plus_1_kernel(a, got, f, out):
    out[:3] = a[...] + got[...]
    out[3] = f[...]


def plus_2_kernel(a, got, f, b, out):
    out[:3] = a[...] + got[:3]
    out[3] = f[...] + got[3]
    out[4] = b[...]


def plus_3_kernel(f, b, got, out):
    out[0] = f[...] + got[3]
    out[1] = b[...] + got[4]


def plus_4_kernel(b, got, out):
    out[...] = b[...] + got[1]


def plus(name, kernel, args, lead, after=()):
    shape = (lead, QUARTER, D) if lead else (QUARTER, D)
    return call(name, kernel, [VMEM] * len(args), shaped(shape), args, after)


def local(
    history, lengths, cotangent, w_qkv, b_qkv, w_out, w_fc1, b_fc1, w_fc2, out_bias,
    norm_gain, norm_bias, mix_gain, mix_in, mix_out, mix_bias,
):
    mg, mi, mb = mix_gain[None], mix_in.T, mix_bias[None]
    w_t = w_qkv.transpose(1, 0, 2)

    normed, rows, g_own, g_send, sum_rows = front(
        lengths, history, cotangent, mg, mi, mix_out, mb, norm_gain, norm_bias
    )
    box_a, slope = fc1(normed, w_fc1, b_fc1[None], g_send)
    mate_a = to_mate(box_a)
    box_b, box_n, sum_hidden, n3_own, n_own = grad_hidden_of(rows, w_fc2, slope, normed)
    mate_b = to_mate(box_b)
    mate_n = to_mate(box_n)
    plan = g_own, box_a, mate_a
    up, down, *a0, g_pair = wgrad("wgrad_a", plan_a, plan, (n_own,), True)
    a1 = to_yz(up, 1, 0), to_yz(down, -1, 0)
    box_c, sum_proj, ring1, ring2, ring3, ring0 = attention(
        lengths, normed, w_t, b_qkv, rows, w_out, rotary(), (up,)
    )
    others = to_x(ring1)
    mate_c = to_mate(box_c)
    plan = n3_own, box_b, mate_b
    up, down, *b0 = wgrad("wgrad_b", plan_b, plan, (sum_proj, mate_n))
    b1 = to_yz(up, 1, 0), to_yz(down, -1, 0)
    f1, f2, f3, f0 = ffn_back(box_b, w_fc1, (up, *a1))
    step = plus("plus_1", plus_1_kernel, (ring2, others, f1), 4)
    others = to_x(step)
    br1, br2, br3, br0 = branches(box_a, box_c, w_out, w_fc2, (step,))
    plan = g_pair, n_own, box_c, mate_c, mate_n
    up, down, *c0 = wgrad("wgrad_c", plan_c, plan, (br1,))
    c1 = to_yz(up, 1, 0), to_yz(down, -1, 0)
    again = front_again(history, cotangent, mg, mi, mix_out, mb, (up,))
    up, down, kept_ab = relay("relay_ab", ((*a0, *a1), (*b0, *b1)), (again[0],))
    ab2 = to_yz(up, 1, 0), to_yz(down, -1, 0)
    step = plus("plus_2", plus_2_kernel, (ring3, others, f2, br1), 5, (up,))
    others = to_x(step)
    up, down, kept_c = relay("relay_c", ((*c0, *c1),), (step,))
    c2 = to_yz(up, 1, 0), to_yz(down, -1, 0)
    step = plus("plus_3", plus_3_kernel, (f3, br2, others), 2, (up,))
    others_f = to_x(step)
    up, down, kept = cross("cross", ((kept_ab, *ab2), (kept_c, *c2)), (step,))
    n1 = to_yz(up, 1, 1), to_yz(down, -1, 1)
    step = plus("plus_4", plus_4_kernel, (br3, others_f), 0, (up,))
    got = to_x(step)
    early = sum_hidden, sum_proj, sum_rows
    rings = ring0, others, f0, others_f
    tiles, *history_parts = front_back(again, rings, mg, mi, mix_out, norm_gain, early, (step,))
    mine = out_rows(lengths, br0, got, again[3], out_bias[None], (tiles,))
    got1, got2, got3 = to_x(mine), to_x(mine, 2), to_x(mine, 3)
    up, down, kept = second("second", kept, *n1, (mine,))
    n2 = to_yz(up, 1, 1), to_yz(down, -1, 1)
    shared = spread(tiles, (up,))
    grad_history = grad_history_of(*history_parts, again[4], (shared,))
    block_out = gathered((got1, got2, got3, mine), (grad_history,))
    places = [(0, D, 0, None), (D, D, 1, None), (2 * D, 512, 2, None)]
    places += [(2 * D + 512 * (c + 1), 512, 3, c) for c in range(3)]
    grad_fc2, grad_fc1, grad_out, grad_qkv = third(
        "third",
        places,
        [shaped((64, D)), shaped((64, D)), shaped((64, 512)), shaped((3, 64, 512))],
        kept,
        *n2,
        (block_out,),
    )
    small = opened(shared, (grad_fc2,))
    g_b_qkv, g_b_fc1, g_b_out, g_gain, g_bias, g_mgain, g_min, g_mout, g_mbias = small
    return (
        block_out,
        grad_history,
        grad_qkv.transpose(1, 0, 2),
        g_b_qkv,
        grad_out.T,
        grad_fc1,
        g_b_fc1[0],
        grad_fc2.T,
        g_b_out[0],
        g_gain,
        g_bias,
        g_mgain[0],
        g_min.T,
        g_mout,
        g_mbias[0],
    )


def solution(mesh):
    in_specs = (
        P(None, "dp", None),
        P("dp"),
        P("dp", None),
        P(None, None, "tensor"),
        P(None, "tensor"),
        P("tensor", None),
        P(None, "tensor"),
        P("tensor"),
        P("tensor", None),
        P(),
        P(),
        P(),
        P(),
        P(),
        P(),
        P(),
    )
    out_specs = (
        P("dp", None),
        P(None, ("dp", "tensor"), None),
        P("dp", None, "tensor"),
        P(),
        P("tensor", "dp"),
        P("dp", "tensor"),
        P(),
        P("tensor", "dp"),
        P(),
        P(),
        P(),
        P(),
        P(),
        P(),
        P(),
    )
    return jax.shard_map(local, mesh=mesh, in_specs=in_specs, out_specs=out_specs, check_vma=False)
```

```python
import functools
import math

import jax
import jax.numpy as jnp
import numpy as np
from jax import lax
from jax.experimental import pallas as pl
from jax.experimental.pallas import tpu as pltpu
from jax.sharding import PartitionSpec as P

D = 2048
HD = 128
ROT = 32
HIST = 9
STREAMS = 4
MIXH = 36
SEQ = 256
QUARTER = 64
F32 = jnp.float32
BF16 = jnp.bfloat16
HIGH = lax.Precision.HIGHEST
ROWS_COLS = (((1,), (1,)), ((), ()))
ROWS_ROWS = (((0,), (0,)), ((), ()))
ALL = ("dp", "tensor")


def place():
    dp = lax.axis_index("dp")
    return dp // 8, (dp // 2) % 4, dp % 2, lax.axis_index("tensor")


def dp_of(y, z, c):
    return ((y % 4) * 4 + z % 4) * 2 + c


def yz_pairs(step, phase):
    out = []
    for y in range(4):
        for z in range(4):
            for c in range(2):
                along_y = c == phase
                to = dp_of(y + step, z, c) if along_y else dp_of(y, z + step, c)
                out.append((dp_of(y, z, c), to))
    return out


def x_pairs(step):
    out = []
    for d in range(32):
        for x in range(4):
            out.append((d * 4 + x, d * 4 + (x + (step if d % 2 == 0 else 4 - step)) % 4))
    return out


def to_yz(a, step, phase):
    return lax.ppermute(a, "dp", yz_pairs(step, phase))


def to_x(a, step=1):
    return lax.ppermute(a, ALL, x_pairs(step))


def to_mate(a):
    return lax.ppermute(a, "dp", [(d, d ^ 1) for d in range(32)])


def x_chunk(c, x, r):
    return jnp.where(c == 0, x - r + 4, x + r) % 4


def gelu_parts(v):
    cdf = 0.5 * (1.0 + lax.erf(v * math.sqrt(0.5)))
    pdf = jnp.exp(-0.5 * v * v) * (1.0 / math.sqrt(2.0 * math.pi))
    return v * cdf, cdf + v * pdf


def rounded(v):
    return v.astype(BF16).astype(F32)


VMEM = pl.BlockSpec(memory_space=pltpu.VMEM)
SMEM = pl.BlockSpec(memory_space=pltpu.SMEM)
ANY = pl.BlockSpec(memory_space=pl.ANY)
HBM = pl.BlockSpec(memory_space=pltpu.HBM)


MIB = {"attention": 12, "grad_hidden": 8, "wgrad_a": 13, "wgrad_b": 13, "wgrad_c": 13, "fc1": 8, "ffn_back": 18, "branches": 18}


COST = {
    "plus_1": 1.0,
    "relay_ab": 8.0,
    "relay_c": 8.0,
    "cross": 3.0,
    "plus_4": 8.0,
    "out_rows": 3.0,
    "second": 3.0,
    "spread": 8.0,
    "gathered": 2.0,
    "third": 1.0,
    "open": 1.0,
}


def call(name, kernel, in_specs, out_shape, args, after=(), scratch=(), grid=(), out_specs=None, mib=None, aliases=None):
    n_in, n_after = len(in_specs), len(after)

    def body(*refs):
        kernel(*refs[:n_in], *refs[n_in + n_after :])

    if out_specs is None:
        out_specs = jax.tree.map(lambda _: VMEM, out_shape)
    return pl.pallas_call(
        body,
        name=name,
        grid=grid,
        in_specs=list(in_specs) + [ANY] * n_after,
        out_specs=out_specs,
        scratch_shapes=list(scratch),
        out_shape=out_shape,
        input_output_aliases=aliases or {},
        compiler_params=pltpu.CompilerParams(vmem_limit_bytes=(mib or MIB.get(name, 16)) * 1024 * 1024),
        cost_estimate=pl.CostEstimate(
            flops=int(COST.get(name, 0.01) * 1e9), bytes_accessed=1, transcendentals=0
        ),
    )(*args, *after)


def held(a):
    return pltpu.with_memory_space_constraint(a, pltpu.HBM)


def whole(shape):
    return pl.BlockSpec(shape, lambda *_: (0,) * len(shape))


def shaped(shape, dtype=F32):
    return jax.ShapeDtypeStruct(shape, dtype)


def split_in_three(w):
    pad = jnp.zeros((4, w.shape[1]), F32)
    parts = []
    for _ in range(3):
        low = w.astype(BF16).astype(F32)
        parts += [low, pad]
        w = w - low
    return jnp.concatenate(parts, 0).astype(BF16)


def mix_of(cur, left, mo, mb):
    wide = cur.astype(F32)
    inv = lax.rsqrt(jnp.mean(wide * wide, -1, keepdims=True) + 1e-06)
    pre = lax.dot_general(cur, left, ROWS_COLS, preferred_element_type=F32)
    pre = inv * (pre[:, 0:36] + pre[:, 40:76] + pre[:, 80:116])
    hid, slope = gelu_parts(pre)
    mw = jnp.dot(hid, mo, precision=HIGH, preferred_element_type=F32) + mb
    return inv, hid, slope, mw


SPREAD = 256


def spreading():
    row = lax.broadcasted_iota(jnp.int32, (MIXH, STREAMS * SPREAD), 0)
    col = lax.broadcasted_iota(jnp.int32, (MIXH, STREAMS * SPREAD), 1)
    at = col % SPREAD
    hit = (row == (col // SPREAD) * HIST + at // 16) & (at < HIST * 16)
    return hit.astype(F32).astype(BF16)


def block_diagonal(mw, spread):
    rows = mw.shape[0]
    row = lax.broadcasted_iota(jnp.int32, (rows, STREAMS * SPREAD), 0)
    col = lax.broadcasted_iota(jnp.int32, (rows, STREAMS * SPREAD), 1)
    same = row % 16 == col % 16
    high = mw.astype(BF16)
    low = (mw - high.astype(F32)).astype(BF16)
    out = []
    for part in (high, low):
        wide = jnp.dot(part, spread, preferred_element_type=F32)
        out.append(jnp.where(same, wide, 0.0).astype(BF16))
    return out


def blend(hist_ref, blocks, stream_ref, rows, start=0):
    totals = []
    for g in range(rows // 16):
        at = slice(g * 16, (g + 1) * 16)
        left = jnp.concatenate(
            [
                part[at, c * SPREAD : c * SPREAD + HIST * 16]
                for part in blocks
                for c in range(STREAMS)
            ],
            0,
        )
        total = None
        for k in range(D // 256):
            cols = slice(k * 256, (k + 1) * 256)
            right = jnp.concatenate(
                [hist_ref[j, pl.ds(start + g * 16, 16), cols] for j in range(HIST)], 0
            )
            res = jnp.dot(left, right, preferred_element_type=F32)
            res = res[: STREAMS * 16] + res[STREAMS * 16 :]
            for c in range(STREAMS):
                stream_ref[c, at, cols] = res[c * 16 : (c + 1) * 16]
            part = res[:, :128] + res[:, 128:]
            total = part if total is None else total + part
        totals.append(jnp.sum(total, -1, keepdims=True))
    return totals


def norm_parts(stream_ref, totals, c, g):
    at = slice(g * 16, (g + 1) * 16)
    mean = totals[g][c * 16 : (c + 1) * 16] * (1.0 / D)
    total = None
    for k in range(D // 256):
        cen = stream_ref[c, at, k * 256 : (k + 1) * 256] - mean
        sq = cen * cen
        part = sq[:, :128] + sq[:, 128:]
        total = part if total is None else total + part
    var = jnp.sum(total, -1, keepdims=True) * (1.0 / D)
    return mean, lax.rsqrt(var + 1e-05)


def front_kernel(
    length, history, cot, mg_in, mi_in, mo_in, mb_in, ng_in, nb_in,
    normed, rows_out, own, send, total,
    hist, mg, mi, mo, mb, ng, nb, left, spread, stream, sems, big_sems,
):
    rows = QUARTER
    small = [
        pltpu.make_async_copy(src, dst, sems.at[n])
        for n, (src, dst) in enumerate(
            ((mg_in, mg), (mi_in, mi), (mo_in, mo), (mb_in, mb), (ng_in, ng), (nb_in, nb))
        )
    ]
    big = [
        pltpu.make_async_copy(
            history.at[:, pl.ds(n * rows, rows), :],
            hist.at[:, pl.ds(n * rows, rows), :],
            big_sems.at[n],
        )
        for n in range(SEQ // rows)
    ]
    for copy in small + big:
        copy.start()
    rows_kernel(length, cot, rows_out, own, send, total)
    for copy in small:
        copy.wait()
    left[...] = split_in_three(mi[...] * mg[...])
    spread[...] = spreading()

    def chunk(n, carry):
        start = pl.multiple_of(n * rows, rows)
        pltpu.make_async_copy(
            history.at[:, pl.ds(start, rows), :],
            hist.at[:, pl.ds(start, rows), :],
            big_sems.at[n],
        ).wait()
        _, _, _, mw = mix_of(hist[HIST - 1, pl.ds(start, rows)], left[...], mo[...], mb[...])
        totals = blend(hist, block_diagonal(mw, spread[...]), stream, rows, start)
        for g in range(rows // 16):
            at = slice(g * 16, (g + 1) * 16)
            for c in range(STREAMS):
                mean, rstd = norm_parts(stream, totals, c, g)
                for k in range(D // 512):
                    cols = slice(k * 512, (k + 1) * 512)
                    cen = stream[c, at, cols] - mean
                    normed[c, pl.ds(start + g * 16, 16), cols] = (
                        cen * rstd * ng[c : c + 1, cols] + nb[c : c + 1, cols]
                    ).astype(BF16)
        return carry

    lax.fori_loop(0, SEQ // rows, chunk, 0)


def front(lengths, history, cotangent, mg, mi, mo, mb, ng, nb):
    return call(
        "front",
        front_kernel,
        [SMEM, HBM, VMEM] + [HBM] * 6,
        [
            shaped((STREAMS, SEQ, D), BF16),
            shaped((SEQ, D), BF16),
            shaped((1024, SEQ), BF16),
            shaped((1024, SEQ)),
            shaped((1, D)),
        ],
        (lengths, held(history), cotangent, *map(held, (mg, mi, mo, mb, ng, nb))),
        (),
        [
            pltpu.VMEM((HIST, SEQ, D), BF16),
            pltpu.VMEM((1, D), F32),
            pltpu.VMEM((MIXH, D), F32),
            pltpu.VMEM((MIXH, MIXH), F32),
            pltpu.VMEM((1, MIXH), F32),
            pltpu.VMEM((STREAMS, D), F32),
            pltpu.VMEM((STREAMS, D), F32),
            pltpu.VMEM((120, D), BF16),
            pltpu.VMEM((MIXH, STREAMS * SPREAD), BF16),
            pltpu.VMEM((STREAMS, QUARTER, D), F32),
            pltpu.SemaphoreType.DMA((6,)),
            pltpu.SemaphoreType.DMA((4,)),
        ],
        mib=24,
    )


def slot(r, h):
    first = jnp.where(r == 0, 6, jnp.where(r == 1, 4, jnp.where(r == 2, 0, 3)))
    second = jnp.where(r == 0, 7, jnp.where(r == 1, 1, jnp.where(r == 2, 2, 5)))
    return jnp.where(h == 0, first, second)


def pick(c):
    row = lax.broadcasted_iota(jnp.int32, (128, 256), 0)
    col = lax.broadcasted_iota(jnp.int32, (128, 256), 1)
    return (col == (row // 64) * 128 + c * 64 + row % 64).astype(F32).astype(BF16)


def arrange(read, own, send):
    y0, z0, c0, _ = place()
    for c, out in ((c0, own), (1 - c0, send)):
        chosen = pick(c)
        for b in range(8):
            flipped = lax.dot_general(chosen, read(b), ROWS_COLS, preferred_element_type=F32)
            for part in range(4):
                y, z, h = b // 2, (b % 2) * 2 + part // 2, part % 2
                dy, dz = (y - y0 + 4) % 4, (z - z0 + 4) % 4
                r1, r2 = jnp.where(c == 0, dy, dz), jnp.where(c == 0, dz, dy)
                inner = slot(r2, h)
                at = pl.multiple_of((slot(r1, inner // 4) * 4 + inner % 4) * 32, 32)
                out[pl.ds(at, 32), :] = flipped[part * 32 : (part + 1) * 32].astype(out.dtype)


def rows_kernel(length, cot, rows_out, own, send, total):
    at = lax.broadcasted_iota(jnp.int32, (SEQ, 1), 0)
    for k in range(8):
        cols = slice(k * 256, (k + 1) * 256)
        g = jnp.where(at < length[0], cot[:, cols].astype(F32), 0.0)
        rows_out[:, cols] = g.astype(BF16)
        total[:, cols] = jnp.sum(g, 0, keepdims=True)
    arrange(lambda b: rows_out[:, b * 256 : (b + 1) * 256], own, send)


def pack(rows, first, second):
    for k in range(4):
        out = first if k < 2 else second
        out[:, (k % 2) * 256 : (k % 2 + 1) * 256] = rows[k * 256 : (k + 1) * 256]


def unpack(first, second):
    pieces = [
        out[:, k * 256 : (k + 1) * 256].astype(BF16) for out in (first, second) for k in range(2)
    ]
    return jnp.concatenate(pieces, 0)


def fc1_kernel(x, w, b, g_send, box, slope):
    for j in range(4):
        cols = slice(j * 512, (j + 1) * 512)
        pre = jnp.dot(x[3], w[:, cols], preferred_element_type=F32) + b[:, cols]
        value, grad = gelu_parts(pre)
        box[j] = rounded(value)
        slope[j] = grad
    pack(g_send, box.at[4], box.at[5])


def fc1(normed, w_fc1, b_fc1, g_send, after=()):
    return call(
        "fc1",
        fc1_kernel,
        [VMEM] * 4,
        [shaped((6, SEQ, 512)), shaped((4, SEQ, 512))],
        (normed, w_fc1, b_fc1, g_send),
        after,
    )


def hidden_kernel(g, w, slope, normed, box, box_n, total, own, own_n, send):
    for j in range(4):
        cols = slice(j * 512, (j + 1) * 512)
        grad = lax.dot_general(g[...], w[cols, :], ROWS_COLS, preferred_element_type=F32)
        low = rounded(grad * slope[j])
        box[j] = low
        total[:, cols] = jnp.sum(low, 0, keepdims=True)
    for c in (3, 0, 1, 2):
        arrange(
            lambda b: normed[c, :, b * 256 : (b + 1) * 256], own if c == 3 else own_n.at[c], send
        )
        out, at = (box, 4) if c == 3 else (box_n, 2 * c)
        pack(send, out.at[at], out.at[at + 1])


def grad_hidden_of(rows, w_fc2, slope, normed, after=()):
    return call(
        "grad_hidden",
        hidden_kernel,
        [VMEM] * 4,
        [
            shaped((6, SEQ, 512)),
            shaped((6, SEQ, 512)),
            shaped((1, D)),
            shaped((1024, SEQ), BF16),
            shaped((3, 1024, SEQ), BF16),
        ],
        (rows, w_fc2, slope, normed),
        after,
        [pltpu.VMEM((1024, SEQ), F32)],
    )


def in_ring_order(read):
    _, _, c, x = place()
    parts = []
    for r in (1, 2, 3, 0):
        at = pl.multiple_of(x_chunk(c, x, r) * QUARTER, QUARTER)
        parts.append(read(pl.ds(at, QUARTER)))
    return jnp.concatenate(parts, 0).astype(BF16)


def to_quarters(res, outs, part, cols):
    for k, out in enumerate(outs):
        out[part, :, cols] = res[k * QUARTER : (k + 1) * QUARTER]


def to_hbm(staged, n, outs, sems):
    copies = [
        pltpu.make_async_copy(
            staged.at[n % 2, pl.ds((k + 1) * QUARTER, QUARTER), :], out, sems.at[n * 3 + k]
        )
        for k, out in enumerate(outs)
    ]
    for copy in copies:
        copy.start()
    return copies


def settle(copies):
    for copy in copies:
        copy.wait()


def quarters(res, outs, cols):
    for k, out in enumerate(outs):
        out[:, cols] = res[k * QUARTER : (k + 1) * QUARTER]


def streamed(w, slots, sems):
    copies = [
        pltpu.make_async_copy(w.at[pl.ds(j * 512, 512), :], slots.at[j], sems.at[j])
        for j in range(4)
    ]
    for copy in copies:
        copy.start()
    return copies


def ffn_back_kernel(box, w, o1, o2, o3, o0, gh, slots, sems):
    copies = streamed(w, slots, sems)
    blocks = [slice(j * 512, (j + 1) * 512) for j in range(4)]
    for j, cols in enumerate(blocks):
        gh[:, cols] = in_ring_order(lambda rows: box[j, rows, :])
    for j, cols in enumerate(blocks):
        copies[j].wait()
        res = lax.dot_general(gh[...], slots[j], ROWS_COLS, preferred_element_type=F32)
        quarters(res, (o1, o2, o3, o0), cols)


STREAM = [
    pltpu.VMEM((SEQ, D), BF16),
    pltpu.VMEM((4, 512, D), BF16),
    pltpu.SemaphoreType.DMA((4,)),
]


def ffn_back(box_b, w_fc1, after=()):
    return call(
        "ffn_back",
        ffn_back_kernel,
        [VMEM, HBM],
        [shaped((QUARTER, D))] * 4,
        (box_b, held(w_fc1)),
        after,
        STREAM,
    )


def branch_kernel(box_a, box_c, wo, w2, o1, o2, o3, o0, act, slots, sems):
    copies = streamed(w2, slots, sems)
    blocks = [slice(j * 512, (j + 1) * 512) for j in range(4)]
    for j, cols in enumerate(blocks):
        act[:, cols] = in_ring_order(lambda rows: box_a[j, rows, :])
    lhs = in_ring_order(lambda rows: box_c[0, rows, :])
    for copy in copies:
        copy.wait()
    for cols in blocks:
        res = jnp.dot(lhs, wo[:, cols], preferred_element_type=F32)
        for j, k in enumerate(blocks):
            res = res + jnp.dot(act[:, k], slots[j, :, cols], preferred_element_type=F32)
        quarters(res, (o1, o2, o3, o0), cols)


def branches(box_a, box_c, w_out, w_fc2, after=()):
    return call(
        "branches",
        branch_kernel,
        [VMEM] * 3 + [HBM],
        [shaped((QUARTER, D))] * 4,
        (box_a, box_c, w_out, held(w_fc2)),
        after,
        STREAM,
    )


def turn(v, cos, lead, tail, sign):
    return v * cos + sign * (pltpu.roll(v, HD - 16, 1) * lead + pltpu.roll(v, 16, 1) * tail)


def attn_kernel(
    length, normed, w, b, rows, wo, cos_ref, lead_ref, tail_ref,
    mid, total, o1, o2, o3, o0, staged, sems,
):
    scale = 1.0 / math.sqrt(HD)
    cos, lead, tail = cos_ref[...], lead_ref[...], tail_ref[...]
    at_q = lax.broadcasted_iota(jnp.int32, (SEQ, SEQ), 0)
    at_k = lax.broadcasted_iota(jnp.int32, (SEQ, SEQ), 1)
    allowed = (at_k <= at_q) & (at_k < length[0])
    for pair in range(2):
        wide = slice(pair * 2 * HD, (pair + 1) * 2 * HD)
        proj = [
            jnp.dot(normed[c], w[c, :, wide], preferred_element_type=F32) + b[c : c + 1, wide]
            for c in range(3)
        ]
        grad_ctx = lax.dot_general(rows[...], wo[wide, :], ROWS_COLS, preferred_element_type=F32)
        for n in range(2):
            cols = slice(n * HD, (n + 1) * HD)
            to = slice((pair * 2 + n) * HD, (pair * 2 + n + 1) * HD)
            q = turn(proj[0][:, cols], cos, lead, tail, 1.0).astype(BF16)
            k = turn(proj[1][:, cols], cos, lead, tail, 1.0).astype(BF16)
            v = proj[2][:, cols].astype(BF16)
            gc = grad_ctx[:, cols].astype(BF16)
            scores = lax.dot_general(q, k, ROWS_COLS, preferred_element_type=F32) * scale
            scores = jnp.where(allowed, scores, -1e30)
            weights = jnp.exp(scores - jnp.max(scores, -1, keepdims=True))
            probs = weights / jnp.sum(weights, -1, keepdims=True)
            low = probs.astype(BF16)
            mid[0, :, to] = rounded(jnp.dot(low, v, preferred_element_type=F32))
            gp = lax.dot_general(gc, v, ROWS_COLS, preferred_element_type=F32)
            gs = (probs * (gp - jnp.sum(probs * gp, -1, keepdims=True))).astype(BF16)
            gv = lax.dot_general(low, gc, ROWS_ROWS, preferred_element_type=F32)
            gq = jnp.dot(gs, k, preferred_element_type=F32) * scale
            gk = lax.dot_general(gs, q, ROWS_ROWS, preferred_element_type=F32) * scale
            grads = (turn(gq, cos, lead, tail, -1.0), turn(gk, cos, lead, tail, -1.0), gv)
            for c in range(3):
                g = rounded(grads[c])
                mid[c + 1, :, to] = g
                total[c : c + 1, to] = jnp.sum(g, 0, keepdims=True)
    sent = []
    for c in range(3):
        if c == 2:
            settle(sent[0])
        lhs = in_ring_order(lambda rows: mid[c + 1, rows, :])
        for j in range(4):
            cols = slice(j * 512, (j + 1) * 512)
            staged[c % 2, :, cols] = lax.dot_general(
                lhs, w[c, cols, :], ROWS_COLS, preferred_element_type=F32
            )
        o1[c] = staged[c % 2, :QUARTER]
        sent.append(to_hbm(staged, c, [out.at[c] for out in (o2, o3, o0)], sems))
    settle(sent[1] + sent[2])


def rotary():
    half = ROT // 2
    position = np.arange(SEQ, dtype=np.float32)
    freq_steps = np.arange(0, ROT, 2, dtype=np.float32) / np.float32(ROT)
    inverse = np.exp(freq_steps * np.float32(-math.log(10000.0)))
    angles = position[:, None] * inverse[None, :]
    cos, sin = np.cos(angles), np.sin(angles)
    wide = np.ones((SEQ, HD), np.float32)
    lead, tail = np.zeros((SEQ, HD), np.float32), np.zeros((SEQ, HD), np.float32)
    wide[:, :half], wide[:, half:ROT] = cos, cos
    lead[:, :half], tail[:, half:ROT] = -sin, sin
    return jnp.asarray(wide), jnp.asarray(lead), jnp.asarray(tail)


def attention(lengths, normed, w_t, b_qkv, rows, w_out, tables, after=()):
    return call(
        "attention",
        attn_kernel,
        [SMEM] + [VMEM] * 8,
        [shaped((4, SEQ, 512)), shaped((3, 512)), shaped((3, QUARTER, D))]
        + [pltpu.HBM((3, QUARTER, D), F32)] * 3,
        (lengths, normed, w_t, b_qkv, rows, w_out, *tables),
        after,
        [pltpu.VMEM((2, SEQ, D), F32), pltpu.SemaphoreType.DMA((9,))],
        out_specs=[VMEM] * 3 + [HBM] * 3,
    )


def wgrad_kernel(plan, n_in, *refs):
    up, down, hop, kept, *saved, staged, sems = refs[n_in:]
    made, last = None, None
    sent = []
    for j, (left, own, first, second, right, mate) in enumerate(plan(refs[:n_in])):
        cols = slice(j * 512, (j + 1) * 512)
        if left != last:
            made = own[...]
            if first is not None:
                made = jnp.concatenate([made, unpack(first, second)], 1)
            for out in saved:
                out[...] = made
        last = left
        both = jnp.concatenate([right[...].astype(BF16), mate[...].astype(BF16)], 0)
        res = jnp.dot(made, both, preferred_element_type=F32)
        up[:, cols] = res[:256]
        down[:, cols] = res[256:512]
        if j >= 2:
            for copy in sent[j - 2]:
                copy.wait()
        staged[j % 2] = res[512:]
        copies = [
            pltpu.make_async_copy(
                staged.at[j % 2, pl.ds(k * 256, 256), :],
                out.at[:, pl.ds(j * 512, 512)],
                sems.at[2 * j + k],
            )
            for k, out in enumerate((hop, kept))
        ]
        for copy in copies:
            copy.start()
        sent.append(copies)
    for copies in sent[2:]:
        for copy in copies:
            copy.wait()


def plan_a(refs):
    own, box, mate = refs
    return [(0, own, mate.at[4], mate.at[5], box.at[j], mate.at[j]) for j in range(4)]


def plan_b(refs):
    own, box, mate = refs
    return [(0, own, mate.at[4], mate.at[5], box.at[j], mate.at[j]) for j in range(4)]


def plan_c(refs):
    g_pair, own, box, mate, mate_n = refs
    out = [(0, g_pair, None, None, box.at[0], mate.at[0])]
    for c in range(3):
        parts = mate_n.at[2 * c], mate_n.at[2 * c + 1]
        out.append((c + 1, own.at[c], *parts, box.at[c + 1], mate.at[c + 1]))
    return out


def wgrad(name, plan, args, after=(), keep=False):
    return call(
        name,
        functools.partial(wgrad_kernel, plan, len(args)),
        [VMEM] * len(args),
        [shaped((256, D))] * 2 + [pltpu.HBM((256, D), F32)] * 2 + [shaped((1024, 512), BF16)] * keep,
        args,
        after,
        [pltpu.VMEM((2, 512, 512), F32), pltpu.SemaphoreType.DMA((8,))],
        out_specs=[VMEM] * 2 + [HBM] * 2 + [VMEM] * keep,
    )


def relay_kernel(*refs):
    *ins, up, down, out = refs
    for n in range(len(ins) // 4):
        hop, kept, up1, down1 = ins[4 * n : 4 * n + 4]
        cols = slice(n * D, (n + 1) * D)
        up[:, cols] = hop[:128] + up1[:128]
        down[:, cols] = hop[128:] + down1[:128]
        out[:128, cols] = kept[:128] + down1[128:]
        out[128:, cols] = kept[128:] + up1[128:]


def relay(name, pieces, after=()):
    args = [a for piece in pieces for a in piece]
    width = len(pieces) * D
    return call(
        name,
        relay_kernel,
        [VMEM] * len(args),
        [shaped((128, width)), shaped((128, width)), shaped((256, width))],
        args,
        after,
    )


def cross_kernel(*refs):
    *ins, up, down, out = refs
    at = 0
    for n in range(len(ins) // 3):
        kept, up2, down2 = ins[3 * n : 3 * n + 3]
        cols = slice(at, at + kept.shape[1])
        at += kept.shape[1]
        up[:, cols] = kept[:64] + up2[:64]
        down[:, cols] = kept[64:128] + up2[64:]
        out[:, cols] = kept[128:] + down2[...]


def cross(name, pieces, after=()):
    args = [a for piece in pieces for a in piece]
    width = sum(piece[0].shape[1] for piece in pieces)
    return call(
        name,
        cross_kernel,
        [VMEM] * len(args),
        [shaped((64, width)), shaped((64, width)), shaped((128, width))],
        args,
        after,
    )


def second_kernel(kept, got_up, got_down, up, down, out):
    up[...] = kept[:32] + got_up[:32]
    down[...] = kept[32:64] + got_down[:32]
    out[:32] = kept[64:96] + got_down[32:]
    out[32:] = kept[96:] + got_up[32:]


def second(name, kept, got_up, got_down, after=()):
    width = kept.shape[1]
    return call(
        name,
        second_kernel,
        [VMEM] * 3,
        [shaped((32, width)), shaped((32, width)), shaped((64, width))],
        (kept, got_up, got_down),
        after,
    )


def third_kernel(places, kept, last_up, last_down, *outs):
    for at, width, n, k in places:
        home = outs[n] if k is None else outs[n].at[k]
        cols = slice(at, at + width)
        home[:32] = kept[:32, cols] + last_up[:, cols]
        home[32:] = kept[32:, cols] + last_down[:, cols]


def third(name, places, out_shape, kept, last_up, last_down, after=()):
    return call(
        name,
        functools.partial(third_kernel, places),
        [VMEM] * 3,
        out_shape,
        (kept, last_up, last_down),
        after,
    )


def again_kernel(
    history, cotangent, mg, mi, mo, mb, hist, cot, hat, resid, wide, keep, left, stream, sems
):
    _, _, _, x = place()
    at = pl.ds(pl.multiple_of(x * QUARTER, QUARTER), QUARTER)
    copies = [
        pltpu.make_async_copy(history.at[:, at, :], hist, sems.at[0]),
        pltpu.make_async_copy(cotangent.at[at, :], cot, sems.at[1]),
    ]
    for copy in copies:
        copy.start()
    left[...] = split_in_three(mi[...] * mg[...])
    for copy in copies:
        copy.wait()
    inv, hid, slope, mw = mix_of(hist[HIST - 1], left[...], mo[...], mb[...])
    keep[:, 0:36] = hid
    keep[:, 128:164] = slope
    keep[:, 256:257] = inv
    for k in range(MIXH):
        wide[k] = jnp.broadcast_to(mw[:, k : k + 1], (QUARTER, 128))
    totals = blend(hist, block_diagonal(mw, spreading()), stream, QUARTER)
    for g in range(QUARTER // 16):
        rows = slice(g * 16, (g + 1) * 16)
        for c in range(STREAMS):
            mean, rstd = norm_parts(stream, totals, c, g)
            keep[rows, 257 + c : 258 + c] = rstd
            hat[c, rows] = (stream[c, rows] - mean) * rstd
    resid[...] = stream[STREAMS - 1]


def front_again(history, cotangent, mg, mi, mo, mb, after=()):
    return call(
        "front_again",
        again_kernel,
        [HBM, HBM] + [VMEM] * 4,
        [
            shaped((HIST, QUARTER, D), BF16),
            shaped((QUARTER, D), BF16),
            shaped((STREAMS, QUARTER, D)),
            shaped((QUARTER, D)),
            shaped((MIXH, QUARTER, 128)),
            shaped((QUARTER, 384)),
        ],
        (held(history), held(cotangent), mg, mi, mo, mb),
        after,
        [
            pltpu.VMEM((120, D), BF16),
            pltpu.VMEM((STREAMS, QUARTER, D), F32),
            pltpu.SemaphoreType.DMA((2,)),
        ],
    )


def back_kernel(
    hist, cot, hat_ref, keep, mine, others, mine_f, others_f, mg_ref, mi_ref, mo_ref, ng_ref,
    sum_hidden, sum_proj, sum_rows, tiles, stream, d_cur, sums, product,
):
    rows = QUARTER
    mg, mi, mo = mg_ref[...], mi_ref[...], mo_ref[...]
    hid, slope, inv = keep[:, 0:36], keep[:, 128:164], keep[:, 256:257]
    for c in range(STREAMS):
        g = mine[c] + others[c] if c < 3 else mine_f[...] + others_f[0]
        hat = hat_ref[c]
        rstd = keep[:, 257 + c : 258 + c]
        sums[36 + c : 37 + c, :] = jnp.sum(g * hat, 0, keepdims=True)
        sums[40 + c : 41 + c, :] = jnp.sum(g, 0, keepdims=True)
        gh = g * ng_ref[c : c + 1]
        ds = rstd * (
            gh - jnp.mean(gh, -1, keepdims=True) - hat * jnp.mean(gh * hat, -1, keepdims=True)
        )
        if c == 3:
            ds = ds + cot[...].astype(F32)
        stream[c] = ds
    for g in range(rows // 16):
        at_rows = slice(g * 16, (g + 1) * 16)
        for c in range(STREAMS):
            for j in range(HIST):
                acc = None
                for k in range(D // 256):
                    cols = slice(k * 256, (k + 1) * 256)
                    term = stream[c, at_rows, cols] * hist[j, at_rows, cols].astype(F32)
                    acc = term if acc is None else acc + term
                product[c * HIST + j, at_rows] = acc[:, :128] + acc[:, 128:]
    lane = lax.broadcasted_iota(jnp.int32, (rows, MIXH), 1)
    gm = jnp.zeros((rows, MIXH), F32)
    for k in range(MIXH):
        gm = jnp.where(lane == k, jnp.sum(product[k], -1, keepdims=True), gm)
    grad_mo = lax.dot_general(hid, gm, ROWS_ROWS, precision=HIGH, preferred_element_type=F32)
    d_pre = slope * lax.dot_general(
        gm, mo, ROWS_COLS, precision=HIGH, preferred_element_type=F32
    )
    low = (inv * d_pre).T
    pad = jnp.zeros((4, rows), F32)
    parts = []
    for _ in range(3):
        part = low.astype(BF16).astype(F32)
        parts += [part, pad]
        low = low - part
    turned_pre = jnp.concatenate(parts, 0).astype(BF16)
    cur_low = hist[HIST - 1]
    three = jnp.dot(turned_pre, cur_low, preferred_element_type=F32)
    outer = three[0:36] + three[40:76] + three[80:116]
    sums[:MIXH, :] = outer * mg
    sums[44:45, :] = jnp.sum(outer * mi, 0, keepdims=True)
    sums[45:56, :] = jnp.zeros((11, D), F32)
    _, _, _, x = place()
    sums[pl.ds(48 + x, 1), :] = sum_hidden[...]
    sums[52:55, pl.ds(pl.multiple_of(x * 512, 512), 512)] = sum_proj[...]
    sums[55:56, :] = jnp.where(x == 0, sum_rows[...], 0.0)
    for g in range(7):
        for t in range(16):
            tiles[g * 16 + t] = sums[g * 8 : (g + 1) * 8, t * 128 : (t + 1) * 128]
    tiles[112:128] = jnp.zeros((16, 8, 128), F32)
    for g in range(4):
        tiles[112 + g, :, :MIXH] = grad_mo[g * 8 : (g + 1) * 8]
    tiles[116, 0:4, :MIXH] = grad_mo[32:36]
    tiles[116, 4:5, :MIXH] = jnp.sum(gm, 0, keepdims=True)
    d_unit = jnp.dot(d_pre, mi * mg, precision=HIGH, preferred_element_type=F32)
    unit = cur_low.astype(F32) * inv
    d_cur[...] = inv * (d_unit - unit * jnp.mean(d_unit * unit, -1, keepdims=True))


def history_kernel(stream, d_cur, wide, grad_hist):
    span = 256
    for g in range(QUARTER // 16):
        at_rows = slice(g * 16, (g + 1) * 16)
        for k in range(D // span):
            cols = slice(k * span, (k + 1) * span)
            ds = [stream[c, at_rows, cols] for c in range(STREAMS)]
            for j in range(HIST):
                acc = d_cur[at_rows, cols] if j == HIST - 1 else None
                for c in range(STREAMS):
                    w = wide[c * HIST + j, at_rows]
                    term = ds[c] * jnp.concatenate([w] * (span // 128), axis=1)
                    acc = term if acc is None else acc + term
                grad_hist[j, at_rows, cols] = acc.astype(BF16)


def front_back(again, rings, mg, mi, mo, ng, early, after=()):
    hist, cot, hat, _, _, keep = again
    return call(
        "front_back",
        back_kernel,
        [VMEM] * 15,
        [shaped((128, 8, 128)), shaped((STREAMS, QUARTER, D)), shaped((QUARTER, D))],
        (hist, cot, hat, keep, *rings, mg, mi, mo, ng, *early),
        after,
        [pltpu.VMEM((56, D), F32), pltpu.VMEM((MIXH, QUARTER, 128), F32)],
    )


def grad_history_of(stream, d_cur, wide, after=()):
    return call(
        "grad_history",
        history_kernel,
        [VMEM] * 3,
        shaped((HIST, QUARTER, D), BF16),
        (stream, d_cur, wide),
        after,
    )


def spread_kernel(each, out):
    out[...] = jnp.broadcast_to(jnp.sum(each[...], 0, keepdims=True), out.shape)


def open_kernel(total, b_qkv, b_fc1, b_out, gain, bias, mgain, m_in, m_out, m_bias, rows):
    for g in range(7):
        for t in range(16):
            rows[g * 8 : (g + 1) * 8, t * 128 : (t + 1) * 128] = total[g * 16 + t]
    m_in[...] = rows[:MIXH]
    gain[...] = rows[36:40]
    bias[...] = rows[40:44]
    mgain[...] = rows[44:45]
    for k in range(4):
        b_fc1[:, k * D : (k + 1) * D] = rows[48 + k : 49 + k]
    b_qkv[...] = rows[52:55]
    b_out[...] = rows[55:56]
    for g in range(4):
        m_out[g * 8 : (g + 1) * 8] = total[112 + g, :, :MIXH]
    m_out[32:36] = total[116, 0:4, :MIXH]
    m_bias[...] = total[116, 4:5, :MIXH]


def spread(tiles, after=()):
    each = lax.all_to_all(tiles, ALL, 0, 0, tiled=True)
    return call("spread", spread_kernel, [VMEM], shaped(tiles.shape), (each,), after)


def opened(mine, after=()):
    total = lax.all_to_all(mine, ALL, 0, 0, tiled=True)
    shapes = [(3, D), (1, 4 * D), (1, D), (STREAMS, D), (STREAMS, D), (1, D), (MIXH, D)]
    shapes += [(MIXH, MIXH), (1, MIXH)]
    return call(
        "open",
        open_kernel,
        [VMEM],
        [shaped(shape) for shape in shapes],
        (total,),
        after,
        [pltpu.VMEM((56, D), F32)],
    )


def out_kernel(length, own, part, resid, bias, out):
    _, _, _, x = place()
    at = lax.broadcasted_iota(jnp.int32, (QUARTER, 1), 0) + x * QUARTER
    valid = jnp.where(at < length[0], 1.0, 0.0)
    out[...] = rounded(resid[...] + valid * (own[...] + part[...] + bias[...]))


def out_rows(lengths, own, part, resid, bias, after=()):
    return call(
        "out_rows",
        out_kernel,
        [SMEM] + [VMEM] * 4,
        shaped((QUARTER, D)),
        (lengths, own, part, resid, bias),
        after,
    )


def gather_kernel(r1, r2, r3, r0, out):
    _, _, c, x = place()
    for r, ref in ((1, r1), (2, r2), (3, r3), (0, r0)):
        at = pl.multiple_of(x_chunk(c, x, r) * QUARTER, QUARTER)
        out[pl.ds(at, QUARTER), :] = ref[...].astype(BF16)


def gathered(parts, after=()):
    return call("gathered", gather_kernel, [VMEM] * 4, shaped((SEQ, D), BF16), parts, after)


def plus_kernel(a, b, out):
    out[...] = a[...] + b[...]


def plus_1_kernel(a, got, f, out):
    out[:3] = a[...] + got[...]
    out[3] = f[...]


def plus_2_kernel(a, got, f, b, out):
    out[:3] = a[...] + got[:3]
    out[3] = f[...] + got[3]
    out[4] = b[...]


def plus_3_kernel(f, b, got, out):
    out[0] = f[...] + got[3]
    out[1] = b[...] + got[4]


def plus_4_kernel(b, got, out):
    out[...] = b[...] + got[1]


def plus(name, kernel, args, lead, after=()):
    shape = (lead, QUARTER, D) if lead else (QUARTER, D)
    return call(name, kernel, [VMEM] * len(args), shaped(shape), args, after)


def local(
    history, lengths, cotangent, w_qkv, b_qkv, w_out, w_fc1, b_fc1, w_fc2, out_bias,
    norm_gain, norm_bias, mix_gain, mix_in, mix_out, mix_bias,
):
    mg, mi, mb = mix_gain[None], mix_in.T, mix_bias[None]
    w_t = w_qkv.transpose(1, 0, 2)

    normed, rows, g_own, g_send, sum_rows = front(
        lengths, history, cotangent, mg, mi, mix_out, mb, norm_gain, norm_bias
    )
    box_a, slope = fc1(normed, w_fc1, b_fc1[None], g_send)
    mate_a = to_mate(box_a)
    box_b, box_n, sum_hidden, n3_own, n_own = grad_hidden_of(rows, w_fc2, slope, normed)
    mate_b = to_mate(box_b)
    mate_n = to_mate(box_n)
    plan = g_own, box_a, mate_a
    up, down, *a0, g_pair = wgrad("wgrad_a", plan_a, plan, (n_own,), True)
    a1 = to_yz(up, 1, 0), to_yz(down, -1, 0)
    box_c, sum_proj, ring1, ring2, ring3, ring0 = attention(
        lengths, normed, w_t, b_qkv, rows, w_out, rotary(), (up,)
    )
    others = to_x(ring1)
    mate_c = to_mate(box_c)
    plan = n3_own, box_b, mate_b
    up, down, *b0 = wgrad("wgrad_b", plan_b, plan, (sum_proj, mate_n))
    b1 = to_yz(up, 1, 0), to_yz(down, -1, 0)
    f1, f2, f3, f0 = ffn_back(box_b, w_fc1, (up, *a1))
    step = plus("plus_1", plus_1_kernel, (ring2, others, f1), 4)
    others = to_x(step)
    plan = g_pair, n_own, box_c, mate_c, mate_n
    up, down, *c0 = wgrad("wgrad_c", plan_c, plan, (step,))
    c1 = to_yz(up, 1, 0), to_yz(down, -1, 0)
    br1, br2, br3, br0 = branches(box_a, box_c, w_out, w_fc2, (up,))
    again = front_again(history, cotangent, mg, mi, mix_out, mb, (br1,))
    up, down, kept_ab = relay("relay_ab", ((*a0, *a1), (*b0, *b1)), (again[0],))
    ab2 = to_yz(up, 1, 0), to_yz(down, -1, 0)
    step = plus("plus_2", plus_2_kernel, (ring3, others, f2, br1), 5, (up,))
    others = to_x(step)
    up, down, kept_c = relay("relay_c", ((*c0, *c1),), (step,))
    c2 = to_yz(up, 1, 0), to_yz(down, -1, 0)
    step = plus("plus_3", plus_3_kernel, (f3, br2, others), 2, (up,))
    others_f = to_x(step)
    up, down, kept = cross("cross", ((kept_ab, *ab2), (kept_c, *c2)), (step,))
    n1 = to_yz(up, 1, 1), to_yz(down, -1, 1)
    step = plus("plus_4", plus_4_kernel, (br3, others_f), 0, (up,))
    got = to_x(step)
    early = sum_hidden, sum_proj, sum_rows
    rings = ring0, others, f0, others_f
    tiles, *history_parts = front_back(again, rings, mg, mi, mix_out, norm_gain, early, (step,))
    mine = out_rows(lengths, br0, got, again[3], out_bias[None], (tiles,))
    got1, got2, got3 = to_x(mine), to_x(mine, 2), to_x(mine, 3)
    up, down, kept = second("second", kept, *n1, (mine,))
    n2 = to_yz(up, 1, 1), to_yz(down, -1, 1)
    shared = spread(tiles, (up,))
    grad_history = grad_history_of(*history_parts, again[4], (shared,))
    block_out = gathered((got1, got2, got3, mine), (grad_history,))
    places = [(0, D, 0, None), (D, D, 1, None), (2 * D, 512, 2, None)]
    places += [(2 * D + 512 * (c + 1), 512, 3, c) for c in range(3)]
    grad_fc2, grad_fc1, grad_out, grad_qkv = third(
        "third",
        places,
        [shaped((64, D)), shaped((64, D)), shaped((64, 512)), shaped((3, 64, 512))],
        kept,
        *n2,
        (block_out,),
    )
    small = opened(shared, (grad_fc2,))
    g_b_qkv, g_b_fc1, g_b_out, g_gain, g_bias, g_mgain, g_min, g_mout, g_mbias = small
    return (
        block_out,
        grad_history,
        grad_qkv.transpose(1, 0, 2),
        g_b_qkv,
        grad_out.T,
        grad_fc1,
        g_b_fc1[0],
        grad_fc2.T,
        g_b_out[0],
        g_gain,
        g_bias,
        g_mgain[0],
        g_min.T,
        g_mout,
        g_mbias[0],
    )


def solution(mesh):
    in_specs = (
        P(None, "dp", None),
        P("dp"),
        P("dp", None),
        P(None, None, "tensor"),
        P(None, "tensor"),
        P("tensor", None),
        P(None, "tensor"),
        P("tensor"),
        P("tensor", None),
        P(),
        P(),
        P(),
        P(),
        P(),
        P(),
        P(),
    )
    out_specs = (
        P("dp", None),
        P(None, ("dp", "tensor"), None),
        P("dp", None, "tensor"),
        P(),
        P("tensor", "dp"),
        P("dp", "tensor"),
        P(),
        P("tensor", "dp"),
        P(),
        P(),
        P(),
        P(),
        P(),
        P(),
        P(),
    )
    return jax.shard_map(local, mesh=mesh, in_specs=in_specs, out_specs=out_specs, check_vma=False)
```
